256 devices in a mesh: dp: 4 (over y), height: 8 (over z_hi, x), tensor: 8 (over z_lo, core).
Axes of the slice: x: 4, y: 4, z: 8 (z_hi: 2, z_lo: 4; z = z_hi * 4 + z_lo), core: 2. Of those that a mesh axis runs over, the one named last changes fastest.
Arguments:
- features: bfloat16 [4, 4, 16, 32, 512], P('dp', None, 'height', None, 'tensor'), may hold values from -6 to 6
- cotangent: bfloat16 [4, 4, 16, 32, 512], P('dp', None, 'height', None, 'tensor'), may hold values from -6 to 6
- conv_one: bfloat16 [27, 512, 512], P(None, 'tensor'), may hold values from -0.0546875 to 0.0546875
- bias_one: float32 [512], P('tensor'), may hold values from -4 to 4
- conv_two: bfloat16 [27, 512, 512], P(None, 'tensor'), may hold values from -0.0546875 to 0.0546875
Outputs:
- grad_features: bfloat16 [4, 4, 16, 32, 512], P('dp', None, 'height', None, 'tensor')
- grad_one: float32 [27, 512, 512], P(None, ('dp', 'height'), 'tensor')
- grad_two: float32 [27, 512, 512], P(None, ('dp', 'height'), 'tensor')
The draws below stay inside these ranges and needn't reach their ends.
All inputs are finite; a program needn't handle non-finite values.
Results may differ from the reference program's by a relative error of at most 0.0052.
Values may be sent and summed in bfloat16 or wider, within the bound.
A program may use at most 128 MiB of HBM per device.

```python
import math
import jax
import jax.numpy as jnp
from jax import lax

C = 512
FRAMES = 4
WIDE = 32
CLIPS = 4
HEIGHT = 16


def steps_of(own_key, extent, cuts, smallest, top_value):
    gain = 1.0
    for position, shards_of in cuts:
        steps = jax.random.uniform(jax.random.fold_in(jax.random.fold_in(own_key, 6), position), (shards_of,), jnp.float32, smallest / len(cuts), top_value / len(cuts))
        gain = gain * jnp.repeat(jnp.exp(steps), extent[position] // shards_of).reshape((-1,) + (1,) * (len(extent) - 1 - position))
    return gain


def centred(own_key, extent, scale, limit, cuts=(), kind=jnp.bfloat16):
    factor_of = steps_of(own_key, extent, cuts, -0.22, 0.18) if cuts else 1.0
    drawn = jax.random.normal(own_key, extent, jnp.float32) * scale * factor_of
    return jnp.minimum(jnp.maximum(drawn, -limit), limit).astype(kind)


def setup_inputs(seed: int = 0) -> dict:
    key_list = jax.random.split(jax.random.key(seed), 6)
    return {
        "features": centred(key_list[0], (CLIPS, FRAMES, HEIGHT, WIDE, C), 1.0, 6.0, ((0, 4), (2, 8), (4, 8))),
        "cotangent": centred(key_list[1], (CLIPS, FRAMES, HEIGHT, WIDE, C), 1.0, 6.0, ((0, 4), (2, 8), (4, 8))),
        "conv_one": centred(key_list[2], (27, C, C), (27 * C) ** -0.5, 0.0546875, ((1, 8),)),
        "bias_one": centred(key_list[3], (C,), 0.7, 4.0, ((0, 8),), jnp.float32),
        "conv_two": centred(key_list[4], (27, C, C), (27 * C) ** -0.5, 0.0546875, ((1, 8),)),
    }


def silu_slope(value):
    sig = jax.nn.sigmoid(value)
    return sig * (1.0 + value * (1.0 - sig))

def forward_patches(extended, frames, row_count, col_count):
    padded = jnp.pad(extended, ((0, 0), (2, 0), (0, 0), (1, 1), (0, 0)))
    windows = [padded[:, shift_time:shift_time + frames, shift_row:shift_row + row_count, shift_col:shift_col + col_count, :] for shift_time in range(3) for shift_row in range(3) for shift_col in range(3)]
    stacked = jnp.stack(windows, axis=-2)
    return stacked.reshape(-1, stacked.shape[-2] * stacked.shape[-1])

def backward_patches(extended, frames, row_count, col_count):
    padded = jnp.pad(extended, ((0, 0), (0, 2), (0, 0), (1, 1), (0, 0)))
    windows = [padded[:, 2 - shift_time:2 - shift_time + frames, 2 - shift_row:2 - shift_row + row_count, 2 - shift_col:2 - shift_col + col_count, :] for shift_time in range(3) for shift_row in range(3) for shift_col in range(3)]
    stacked = jnp.stack(windows, axis=-2)
    return stacked.reshape(-1, stacked.shape[-2] * stacked.shape[-1])

def pad_rows(value):
    return jnp.pad(value, ((0, 0), (0, 0), (1, 1), (0, 0), (0, 0)))

def contract_rows(left, right):
    return lax.dot_general(left, right, (((0,), (0,)), ((), ())), preferred_element_type=jnp.float32)

def reference(features, cotangent, conv_one, bias_one, conv_two):
    channels = conv_one.shape[2]
    frames, row_count, col_count = (FRAMES, HEIGHT, WIDE)
    grad_scale = 1.0 / math.sqrt(CLIPS * FRAMES * HEIGHT * WIDE)
    ahead_one = jnp.transpose(conv_one, (0, 2, 1)).reshape(-1, channels)
    flip_one = conv_one.reshape(-1, channels)
    flip_two = conv_two.reshape(-1, channels)

    def one_clip(clip_pair):
        clip_feat = clip_pair[0][None]
        clip_cot = clip_pair[1][None]
        shape_full = clip_feat.shape
        act_one = jax.nn.silu(clip_feat.astype(jnp.float32)).astype(jnp.bfloat16)
        patch_one = forward_patches(pad_rows(act_one), frames, row_count, col_count)
        preact = jnp.dot(patch_one, ahead_one, preferred_element_type=jnp.float32).reshape(shape_full) + bias_one
        act_two = jax.nn.silu(preact).astype(jnp.bfloat16)
        patch_two = forward_patches(pad_rows(act_two), frames, row_count, col_count)
        cot_rows = clip_cot.reshape(-1, channels)
        clip_two = contract_rows(patch_two, cot_rows).reshape(27, channels, channels)
        back_two = jnp.dot(backward_patches(pad_rows(clip_cot), frames, row_count, col_count), flip_two, preferred_element_type=jnp.float32).reshape(shape_full)
        grad_pre = (back_two * silu_slope(preact)).astype(jnp.bfloat16)
        clip_one = contract_rows(patch_one, grad_pre.reshape(-1, channels)).reshape(27, channels, channels)
        back_one = jnp.dot(backward_patches(pad_rows(grad_pre), frames, row_count, col_count), flip_one, preferred_element_type=jnp.float32).reshape(shape_full)
        grad_in = (clip_cot.astype(jnp.float32) + back_one * silu_slope(clip_feat.astype(jnp.float32))).astype(jnp.bfloat16)
        return (grad_in[0], clip_one, clip_two)
    grad_in, per_one, per_two = lax.map(one_clip, (features, cotangent))
    grad_one = lax.optimization_barrier(jnp.sum(per_one, axis=0)) * grad_scale
    grad_two = lax.optimization_barrier(jnp.sum(per_two, axis=0)) * grad_scale
    return (grad_in, grad_one, grad_two)
```

```python
import math

import jax
import jax.numpy as jnp
from jax import lax
from jax.experimental import pallas as pl
from jax.experimental.pallas import tpu as pltpu
from jax.sharding import PartitionSpec as P

BF = jnp.bfloat16
F32 = jnp.float32
MESH = pl.DeviceIdType.MESH

NX, NZ, NY, NT = 4, 2, 4, 8
TAPS = [(a, b) for a in range(3) for b in range(3)]


def iota(shape, dim):
    return lax.broadcasted_iota(jnp.int32, shape, dim)


def swap(v):
    return pltpu.roll(v, 64, 1)


def low_lane(v):
    return iota(v.shape, 1) < 64


def next_column(v):
    rows = v.shape[0]
    edge = jnp.where(low_lane(v), swap(pltpu.roll(v, 15, 0)), 0.0)
    return jnp.where(iota(v.shape, 0) % 16 == 15, edge, pltpu.roll(v, rows - 1, 0))


def prev_column(v):
    rows = v.shape[0]
    edge = jnp.where(low_lane(v), 0.0, swap(pltpu.roll(v, rows - 15, 0)))
    return jnp.where(iota(v.shape, 0) % 16 == 0, edge, pltpu.roll(v, 1, 0))


def merge(first, second):
    return jnp.where(low_lane(first), first, swap(second))


def merge_high(first, second):
    return jnp.where(low_lane(first), swap(first), second)


def slope(v):
    sig = jax.nn.sigmoid(v)
    return sig * (1.0 + v * (1.0 - sig))


def silu(v):
    return v * jax.nn.sigmoid(v)


def dot(left, right, dims):
    return lax.dot_general(left, right, (dims, ((), ())), preferred_element_type=F32)


def kernel(
    feat, cot, bias, w1_hbm, w2_hbm,
    out_in, out_one, out_two,
    w1, w2, xa, xn, gc, gp, g3c, g3p, part, se, re, sh, rh, acc,
    xs1, xs2, xt1, xt2, sy1, sy2, ry1, ry2, sz1, sz2, rz1, rz2, oz1, oz2,
    featp, cotp,
    w_sem, a_send, a_recv, hu_send, hd_send, hu_recv, hd_recv,
    c_send, c_recv, ce_send, ce_recv, p_send, p_recv, pe_send, pe_recv,
    e_send, e_recv, h_send, h_recv, x1_send, x1_recv, x2_send, x2_recv,
    y1_send, y1_recv, y2_send, y2_recv, z1_send, z1_recv, z2_send, z2_recv,
):
    d = lax.axis_index("dp")
    h = lax.axis_index("height")
    t = lax.axis_index("tensor")
    x = h % NX
    z = h // NX
    mine = x * NT + t

    def remote(src, dst, ssem, rsem, where):
        return pltpu.make_async_remote_copy(
            src_ref=src, dst_ref=dst, send_sem=ssem, recv_sem=rsem,
            device_id=where, device_id_type=MESH,
        )

    copy_w2 = pltpu.make_async_copy(w2_hbm, w2, w_sem.at[0])
    copy_w1 = pltpu.make_async_copy(w1_hbm, w1, w_sem.at[1])
    copy_w2.start()
    copy_w1.start()

    barrier = pltpu.get_barrier_semaphore()

    def greet_slab(k, carry):
        other = (mine + k) % (NX * NT)
        pl.semaphore_signal(
            barrier, inc=1, device_id=(d, z * NX + other // NT, other % NT),
            device_id_type=MESH)
        return carry

    lax.fori_loop(1, NX * NT, greet_slab, 0)
    for k in range(1, NY):
        pl.semaphore_signal(
            barrier, inc=1, device_id=((d + k) % NY, h, t), device_id_type=MESH)
    for k in range(NX):
        pl.semaphore_signal(
            barrier, inc=1, device_id=(d, (1 - z) * NX + k, t), device_id_type=MESH)

    for r in range(2):
        for f in range(4):
            v = feat[0, f, r].astype(F32)
            v = jnp.concatenate([v[:16], v[16:]], axis=-1)
            featp[r, f] = v
            xa[t, 1 + r, f] = silu(v).astype(BF)
            c = cot[0, f, r].astype(F32)
            c = jnp.concatenate([c[:16], c[16:]], axis=-1)
            cotp[r, f] = c
            gc[2 * x + 1 + r, f] = c.astype(BF)

    zero_row = jnp.zeros((4, 16, 128), BF)
    for ref in (gc, gp):
        @pl.when(z == 0)
        def _():
            ref[0] = zero_row

        @pl.when(z == 1)
        def _():
            ref[9] = zero_row

    @pl.when(h == 0)
    def _():
        for k in range(NT):
            xa[k, 0] = zero_row

    @pl.when(h == NX * NZ - 1)
    def _():
        for k in range(NT):
            xa[k, 3] = zero_row

    pl.semaphore_wait(barrier, NX * NT - 1 + NY - 1 + NX)

    def gather_act(k):
        return remote(xa.at[t, pl.ds(1, 2)], xa.at[t, pl.ds(1, 2)],
                      a_send.at[k - 1], a_recv.at[t], (d, h, (t + k) % NT))

    def gather_rows(ref, ssem, rsem, k):
        rows = ref.at[pl.ds(2 * x + 1, 2)]
        return remote(rows, rows, ssem.at[k - 1], rsem.at[x],
                      (d, z * NX + (x + k) % NX, t))

    def edge_up(ref, ssem, rsem, k):
        return remote(ref.at[8], ref.at[0], ssem.at[k], rsem.at[0], (d, NX + k, t))

    def edge_down(ref, ssem, rsem, k):
        return remote(ref.at[1], ref.at[9], ssem.at[k], rsem.at[0], (d, k, t))

    def on_edges(ref, ssem, rsem, act):
        @pl.when(h == NX - 1)
        def _():
            for k in range(NX):
                act(edge_up(ref, ssem, rsem, k))

        @pl.when(h == NX)
        def _():
            for k in range(NX):
                act(edge_down(ref, ssem, rsem, k))

    def start(copy):
        copy.start()

    def wait_send(copy):
        copy.wait_send()

    def send_rows(ref, ssem, rsem, esend, erecv):
        for k in (1, 3, 2):
            gather_rows(ref, ssem, rsem, k).start()
        on_edges(ref, esend, erecv, start)

    def await_rows(ref, ssem, rsem, esend, erecv):
        for k in range(1, NX):
            other = (x + k) % NX
            rows = ref.at[pl.ds(2 * other + 1, 2)]
            remote(rows, rows, ssem.at[0], rsem.at[other], (d, h, t)).wait_recv()
        edge = ref.at[0]
        remote(edge, edge, esend.at[0], erecv.at[0], (d, h, t)).wait_recv()

    def finish_rows(ref, ssem, rsem, esend, erecv):
        for k in range(1, NX):
            gather_rows(ref, ssem, rsem, k).wait_send()
        on_edges(ref, esend, erecv, wait_send)

    def scatter(src, dst, ssem, rsem, k):
        other = (t + k) % NT
        return remote(src.at[other], dst.at[t], ssem.at[k - 1], rsem.at[t],
                      (d, h, other))

    def await_block(dst, ssem, rsem, k):
        other = (t + k) % NT
        remote(dst.at[other], dst.at[other], ssem.at[0], rsem.at[other],
               (d, h, t)).wait_recv()

    def send_act(src, dst, ssem, rsem, k):
        other = (mine + k) % (NX * NT)
        return remote(src.at[other // NT], dst.at[x, t], ssem.at[k - 1],
                      rsem.at[mine], (d, z * NX + other // NT, other % NT))

    def send_acts(src, dst, ssem, rsem):
        def step(k, carry):
            send_act(src, dst, ssem, rsem, k).start()
            return carry
        lax.fori_loop(1, NX * NT, step, 0)

    def await_acts(dst, ssem, rsem):
        def step(k, carry):
            other = (mine + k) % (NX * NT)
            block = dst.at[other // NT, other % NT]
            remote(block, block, ssem.at[0], rsem.at[other], (d, h, t)).wait_recv()
            return carry
        lax.fori_loop(1, NX * NT, step, 0)

    def finish_acts(src, dst, ssem, rsem):
        def step(k, carry):
            send_act(src, dst, ssem, rsem, k).wait_send()
            return carry
        lax.fori_loop(1, NX * NT, step, 0)

    def spread(rows, dst):
        v = rows[...].astype(F32).reshape(640, 128)
        up, down = next_column(v), prev_column(v)
        nothing = jnp.zeros_like(v)
        pieces = (
            (merge(up, v), merge(down, nothing)),
            (merge_high(up, v), merge_high(down, nothing)),
        )
        for half in range(2):
            for side in range(2):
                dst[half, :, 0:4, :, 128 * side:128 * side + 128] = (
                    pieces[half][side].astype(BF).reshape(10, 4, 16, 128))
            dst[half, :, 4:6] = jnp.zeros((10, 2, 16, 256), BF)

    def transposed_conv(g3, w, dst):
        for a, b in sorted(TAPS, reverse=True):
            n = 2 + a
            left = g3[:, pl.ds(2 * x + 2 - b, 2), 2 - a:4, :, 0:192]
            tap = 3 * (3 * a + b)
            right = w[tap:tap + 3].reshape(192, 512)
            v = dot(left.reshape(64 * n, 192), right, ((1,), (0,)))
            v = v.reshape(2, 2, n, 16, 512)
            if (a, b) == (2, 2):
                part[...] = v
            else:
                part[:, :, 0:n] = part[:, :, 0:n] + v

    def split_part(dst):
        for p in range(4):
            low = part[0, :, :, :, 128 * p:128 * p + 128].reshape(128, 128)
            high = part[1, :, :, :, 128 * p:128 * p + 128].reshape(128, 128)
            dst[2 * p] = merge(low, high).astype(BF).reshape(2, 4, 16, 128)
            dst[2 * p + 1] = merge_high(low, high).astype(BF).reshape(2, 4, 16, 128)

    def transposed(packed, src, dst):
        v = jnp.transpose(packed)
        v = jnp.concatenate([v[:64], v[64:]], axis=1).astype(BF)
        src[...] = v.reshape(4, 16, 256)
        dst[x, t] = src[x]

    def kernel_grad(xt, g3, sy):
        for a, b in TAPS:
            total = None
            for s in range(NX):
                left = xt[s].reshape(128, 256)
                right = g3[:, 2 * s + 2 - b:2 * s + 4 - b, 2 - a:6 - a, :, 0:192]
                v = dot(left, right.reshape(256, 192), ((1,), (0,)))
                total = v if total is None else total + v
            sy[:, 3 * a + b] = total.astype(BF).reshape(8, 16, 192)

    def send_y(sy, ry, ssem, rsem, k):
        other = (d + k) % NY
        return remote(sy.at[pl.ds(2 * other, 2)], ry.at[d], ssem.at[k - 1],
                      rsem.at[d], (other, h, t))

    def await_y(ry, ssem, rsem):
        for k in range(1, NY):
            other = (d + k) % NY
            remote(ry.at[other], ry.at[other], ssem.at[0], rsem.at[other],
                   (d, h, t)).wait_recv()

    def send_z(sz, rz, ssem, rsem):
        return remote(sz, rz, ssem.at[0], rsem.at[0], (d, (1 - z) * NX + x, t))

    def sum_y(sy, ry, which):
        total = sy[2 * d + which].astype(F32)
        for k in range(1, NY):
            total = total + ry[(d + k) % NY, which].astype(F32)
        return total

    scale = 1.0 / math.sqrt(4 * 4 * 16 * 32)

    def write_grad(oz, rz, out):
        v = (oz[...] + rz[...].astype(F32)) * scale
        for k in range(9):
            for e in range(3):
                out[3 * k + e] = v[k, :, 64 * e:64 * e + 64]

    send_rows(gc, c_send, c_recv, ce_send, ce_recv)
    for k in (1, 7, 2, 6, 3, 5, 4):
        gather_act(k).start()

    await_rows(gc, c_send, c_recv, ce_send, ce_recv)
    spread(gc, g3c)
    copy_w2.wait()
    transposed_conv(g3c, w2, part)
    split_part(se)
    for k in range(1, NT):
        scatter(se, re, e_send, e_recv, k).start()

    def halo_up(k):
        return remote(xa.at[k, 1], xa.at[k, 3], hu_send.at[k], hu_recv.at[k],
                      (d, h - 1, t))

    def halo_down(k):
        return remote(xa.at[k, 2], xa.at[k, 0], hd_send.at[k], hd_recv.at[k],
                      (d, h + 1, t))

    for k in (0, 1, 7, 2, 6, 3, 5, 4):
        other = (t + k) % NT
        if k:
            rows = xa.at[other, pl.ds(1, 2)]
            remote(rows, rows, a_send.at[0], a_recv.at[other], (d, h, t)).wait_recv()

        @pl.when(h > 0)
        def _():
            halo_up(other).start()

        @pl.when(h < NX * NZ - 1)
        def _():
            halo_down(other).start()

    transposed(xa[t, 1:3].astype(F32).reshape(128, 128), xs1, xt1)
    send_acts(xs1, xt1, x1_send, x1_recv)

    @pl.when(h < NX * NZ - 1)
    def _():
        for k in range(NT):
            remote(xa.at[k, 3], xa.at[k, 3], hu_send.at[0], hu_recv.at[k],
                   (d, h, t)).wait_recv()

    @pl.when(h > 0)
    def _():
        for k in range(NT):
            remote(xa.at[k, 0], xa.at[k, 0], hd_send.at[0], hd_recv.at[k],
                   (d, h, t)).wait_recv()

    for p in range(4):
        first = xa[2 * p].astype(F32).reshape(256, 128)
        second = xa[2 * p + 1].astype(F32).reshape(256, 128)
        xn[0, :, :, :, 128 * p:128 * p + 128] = (
            merge(first, second).astype(BF).reshape(4, 4, 16, 128))
        xn[1, :, :, :, 128 * p:128 * p + 128] = (
            merge_high(first, second).astype(BF).reshape(4, 4, 16, 128))

    copy_w1.wait()
    acc[...] = jnp.zeros_like(acc)
    for a, b in TAPS:
        n = 2 + a
        left = xn[:, b:b + 2, 0:n].reshape(64 * n, 512)
        tap = 3 * (3 * a + b)
        right = w1[tap:tap + 3].reshape(192, 512)
        v = dot(left, right, ((1,), (1,))).reshape(2, 2, n, 16, 192)
        acc[:, :, 2 - a:4, :, 0:192] = acc[:, :, 2 - a:4, :, 0:192] + v
    low0 = acc[0, :, :, :, 0:128].reshape(128, 128)
    low1 = acc[0, :, :, :, 128:256].reshape(128, 128)
    high0 = acc[1, :, :, :, 0:128].reshape(128, 128)
    high1 = acc[1, :, :, :, 128:256].reshape(128, 128)
    wide_bias = jnp.concatenate([bias[...], bias[...]], axis=1)
    preact = (prev_column(merge(low0, high0)) + merge_high(low0, high0)
              + next_column(merge(low1, high1)) + wide_bias)
    act_two = silu(preact).astype(BF).astype(F32)

    for k in range(1, NT):
        await_block(re, e_send, e_recv, k)
    back = se[t].astype(F32)
    for k in range(1, NT):
        back = back + re[(t + k) % NT].astype(F32)
    grad_pre = back.reshape(128, 128) * slope(preact)
    gp[pl.ds(2 * x + 1, 2)] = grad_pre.astype(BF).reshape(2, 4, 16, 128)
    send_rows(gp, p_send, p_recv, pe_send, pe_recv)
    transposed(act_two, xs2, xt2)
    send_acts(xs2, xt2, x2_send, x2_recv)

    await_rows(gp, p_send, p_recv, pe_send, pe_recv)
    spread(gp, g3p)
    transposed_conv(g3p, w1, part)
    split_part(sh)
    for k in range(1, NT):
        scatter(sh, rh, h_send, h_recv, k).start()

    await_acts(xt1, x1_send, x1_recv)
    kernel_grad(xt1, g3p, sy1)
    for k in (1, 3, 2):
        send_y(sy1, ry1, y1_send, y1_recv, k).start()
    await_acts(xt2, x2_send, x2_recv)
    kernel_grad(xt2, g3c, sy2)
    for k in (1, 3, 2):
        send_y(sy2, ry2, y2_send, y2_recv, k).start()

    await_y(ry1, y1_send, y1_recv)
    sz1[...] = sum_y(sy1, ry1, 1 - z).astype(BF)
    send_z(sz1, rz1, z1_send, z1_recv).start()
    oz1[...] = sum_y(sy1, ry1, z)

    for k in range(1, NT):
        await_block(rh, h_send, h_recv, k)
    back = sh[t].astype(F32)
    for k in range(1, NT):
        back = back + rh[(t + k) % NT].astype(F32)
    grad_in = cotp[...] + back * slope(featp[...])
    for r in range(2):
        for f in range(4):
            out_in[0, f, r, 0:16] = grad_in[r, f, :, 0:64].astype(BF)
            out_in[0, f, r, 16:32] = grad_in[r, f, :, 64:128].astype(BF)

    await_y(ry2, y2_send, y2_recv)
    sz2[...] = sum_y(sy2, ry2, 1 - z).astype(BF)
    send_z(sz2, rz2, z2_send, z2_recv).start()
    oz2[...] = sum_y(sy2, ry2, z)

    send_z(sz1, rz1, z1_send, z1_recv).wait_recv()
    write_grad(oz1, rz1, out_one)
    send_z(sz2, rz2, z2_send, z2_recv).wait_recv()
    write_grad(oz2, rz2, out_two)

    for k in range(1, NT):
        gather_act(k).wait_send()
        scatter(se, re, e_send, e_recv, k).wait_send()
        scatter(sh, rh, h_send, h_recv, k).wait_send()

    @pl.when(h > 0)
    def _():
        for k in range(NT):
            halo_up(k).wait_send()

    @pl.when(h < NX * NZ - 1)
    def _():
        for k in range(NT):
            halo_down(k).wait_send()

    finish_rows(gc, c_send, c_recv, ce_send, ce_recv)
    finish_rows(gp, p_send, p_recv, pe_send, pe_recv)
    finish_acts(xs1, xt1, x1_send, x1_recv)
    finish_acts(xs2, xt2, x2_send, x2_recv)
    for k in range(1, NY):
        send_y(sy1, ry1, y1_send, y1_recv, k).wait_send()
        send_y(sy2, ry2, y2_send, y2_recv, k).wait_send()
    send_z(sz1, rz1, z1_send, z1_recv).wait_send()
    send_z(sz2, rz2, z2_send, z2_recv).wait_send()


def local(features, cotangent, conv_one, bias_one, conv_two):
    vmem = pl.BlockSpec(memory_space=pltpu.VMEM)
    hbm = pl.BlockSpec(memory_space=pl.ANY)
    dma = pltpu.SemaphoreType.DMA
    block = (2, 4, 16, 128)
    scratch = [
        pltpu.VMEM((27, 64, 512), BF), pltpu.VMEM((27, 64, 512), BF),
        pltpu.VMEM((8, 4, 4, 16, 128), BF), pltpu.VMEM((2, 4, 4, 16, 512), BF),
        pltpu.VMEM((10, 4, 16, 128), BF), pltpu.VMEM((10, 4, 16, 128), BF),
        pltpu.VMEM((2, 10, 6, 16, 256), BF), pltpu.VMEM((2, 10, 6, 16, 256), BF),
        pltpu.VMEM((2, 2, 4, 16, 512), F32),
        pltpu.VMEM((8,) + block, BF), pltpu.VMEM((8,) + block, BF),
        pltpu.VMEM((8,) + block, BF), pltpu.VMEM((8,) + block, BF),
        pltpu.VMEM((2, 2, 4, 16, 256), F32),
        pltpu.VMEM((4, 16, 256), BF), pltpu.VMEM((4, 16, 256), BF),
        pltpu.VMEM((4, 8, 16, 256), BF), pltpu.VMEM((4, 8, 16, 256), BF),
        pltpu.VMEM((8, 9, 16, 192), BF), pltpu.VMEM((8, 9, 16, 192), BF),
        pltpu.VMEM((4, 2, 9, 16, 192), BF), pltpu.VMEM((4, 2, 9, 16, 192), BF),
        pltpu.VMEM((9, 16, 192), BF), pltpu.VMEM((9, 16, 192), BF),
        pltpu.VMEM((9, 16, 192), BF), pltpu.VMEM((9, 16, 192), BF),
        pltpu.VMEM((9, 16, 192), F32), pltpu.VMEM((9, 16, 192), F32),
        pltpu.VMEM(block, F32), pltpu.VMEM(block, F32),
        dma((2,)), dma((7,)), dma((8,)),
        dma((8,)), dma((8,)), dma((8,)), dma((8,)),
        dma((3,)), dma((4,)), dma((4,)), dma((1,)),
        dma((3,)), dma((4,)), dma((4,)), dma((1,)),
        dma((7,)), dma((8,)), dma((7,)), dma((8,)),
        dma((31,)), dma((32,)), dma((31,)), dma((32,)),
        dma((3,)), dma((4,)), dma((3,)), dma((4,)),
        dma((1,)), dma((1,)), dma((1,)), dma((1,)),
    ]
    return pl.pallas_call(
        kernel,
        out_shape=(
            jax.ShapeDtypeStruct((1, 4, 2, 32, 64), BF),
            jax.ShapeDtypeStruct((27, 16, 64), F32),
            jax.ShapeDtypeStruct((27, 16, 64), F32),
        ),
        in_specs=[vmem, vmem, vmem, hbm, hbm],
        out_specs=(vmem, vmem, vmem),
        scratch_shapes=scratch,
        compiler_params=pltpu.CompilerParams(
            collective_id=0, has_side_effects=True, vmem_limit_bytes=40 * 1024 * 1024
        ),
    )(features, cotangent, bias_one.reshape(1, -1), conv_one, conv_two)


def solution(mesh):
    in_specs = (
        P("dp", None, "height", None, "tensor"),
        P("dp", None, "height", None, "tensor"),
        P(None, "tensor", None),
        P("tensor"),
        P(None, "tensor", None),
    )
    out_specs = (
        P("dp", None, "height", None, "tensor"),
        P(None, ("dp", "height"), "tensor"),
        P(None, ("dp", "height"), "tensor"),
    )
    return jax.shard_map(local, mesh=mesh, in_specs=in_specs, out_specs=out_specs, check_vma=False)
```

```python
import math

import jax
import jax.numpy as jnp
from jax import lax
from jax.experimental import pallas as pl
from jax.experimental.pallas import tpu as pltpu
from jax.sharding import PartitionSpec as P

BF = jnp.bfloat16
F32 = jnp.float32
MESH = pl.DeviceIdType.MESH

NX, NZ, NY, NT = 4, 2, 4, 8
SENDS, RECVS = 136, 160
TAPS = [(a, b) for a in range(3) for b in range(3)]


def iota(shape, dim):
    return lax.broadcasted_iota(jnp.int32, shape, dim)


def swap(v):
    return pltpu.roll(v, 64, 1)


def low_lane(v):
    return iota(v.shape, 1) < 64


def next_column(v):
    rows = v.shape[0]
    edge = jnp.where(low_lane(v), swap(pltpu.roll(v, 15, 0)), 0.0)
    return jnp.where(iota(v.shape, 0) % 16 == 15, edge, pltpu.roll(v, rows - 1, 0))


def prev_column(v):
    rows = v.shape[0]
    edge = jnp.where(low_lane(v), 0.0, swap(pltpu.roll(v, rows - 15, 0)))
    return jnp.where(iota(v.shape, 0) % 16 == 0, edge, pltpu.roll(v, 1, 0))


def merge(first, second):
    return jnp.where(low_lane(first), first, swap(second))


def merge_high(first, second):
    return jnp.where(low_lane(first), swap(first), second)


def slope(v):
    sig = jax.nn.sigmoid(v)
    return sig * (1.0 + v * (1.0 - sig))


def silu(v):
    return v * jax.nn.sigmoid(v)


def dot(left, right, dims):
    return lax.dot_general(left, right, (dims, ((), ())), preferred_element_type=F32)


def kernel(
    feat_hbm, cot_hbm, bias_hbm, w1_hbm, w2_hbm,
    in_hbm, one_hbm, two_hbm,
    feat, cot, bias, w1, w2, xa, xn, cn, gn, gc, gp, g3n, g3c, g3p, part, acc,
    own, e1, e1r, e2, e2r, h1, h1r, h2, h2r,
    xs1, xs2, xr2, xt1, xt2, sf1, sf2, sy1, sy2, ry1, ry2,
    featp, cotp, out_in, out_one, out_two, in_sem, out_sem, send_sem, recv_sem,
):
    d = lax.axis_index("dp")
    h = lax.axis_index("height")
    t = lax.axis_index("tensor")
    x = h % NX
    z = h // NX
    k = t // 2
    c = t % 2
    home = c == z
    partner = (1 - z) * NX + x
    here = (d, h, t)
    sibling = (d, h, 2 * k + 1 - c)

    copies = [
        pltpu.make_async_copy(src, dst, in_sem.at[i]) for i, (src, dst) in enumerate(
            [(feat_hbm, feat), (cot_hbm, cot), (bias_hbm, bias), (w2_hbm, w2), (w1_hbm, w1)])
    ]
    for copy in copies:
        copy.start()

    counts = {"send": 0, "recv": 0}

    def reserve(kind, n):
        base = counts[kind]
        counts[kind] = base + n
        return base

    def remote(src, dst, s, r, where):
        return pltpu.make_async_remote_copy(
            src_ref=src, dst_ref=dst, send_sem=send_sem.at[s], recv_sem=recv_sem.at[r],
            device_id=where, device_id_type=MESH,
        )

    unfinished = []

    def post(src, dst, r, where, when=None):
        s = reserve("send", 1)

        def make():
            return remote(src, dst, s, r, where)

        def begin():
            make().start()

        def finish():
            make().wait_send()

        if when is None:
            begin()
        else:
            pl.when(when)(begin)
        unfinished.append((finish, when))

    def await_into(dst, r):
        remote(dst, dst, 0, r, here).wait_recv()

    barrier = pltpu.get_barrier_semaphore()

    def greet(where):
        pl.semaphore_signal(barrier, inc=1, device_id=where, device_id_type=MESH)

    for i in range(NX):
        for j in range(4):
            if i or j:
                greet((d, z * NX + (x + i) % NX, 2 * ((k + j) % 4) + c))
        greet((d, (1 - z) * NX + i, t))
    for i in range(1, NY):
        greet(((d + i) % NY, h, t))
    greet(sibling)

    copies[0].wait()
    copies[1].wait()
    copies[2].wait()
    for r in range(2):
        for f in range(4):
            v = feat[0, f, r].astype(F32)
            v = jnp.concatenate([v[:16], v[16:]], axis=-1)
            featp[r, f] = v
            xa[c, k, 1 + r, f] = silu(v).astype(BF)
            v = cot[0, f, r].astype(F32)
            v = jnp.concatenate([v[:16], v[16:]], axis=-1)
            cotp[r, f] = v
            cn[1 + r, f] = v.astype(BF)
            gc[2 * h + r, f] = v.astype(BF)

    zero_row = jnp.zeros((4, 16, 128), BF)
    @pl.when(h == 0)
    def _():
        for i in range(2):
            for j in range(4):
                xa[i, j, 0] = zero_row
        cn[0] = zero_row
        gn[0] = zero_row

    @pl.when(h == NX * NZ - 1)
    def _():
        for i in range(2):
            for j in range(4):
                xa[i, j, 3] = zero_row
        cn[3] = zero_row
        gn[3] = zero_row

    for ref in (g3c, g3p):
        for i in range(2):
            for j in (0, 17):
                ref[i, j] = jnp.zeros((6, 16, 256), BF)
            for j in (4, 5):
                ref[i, :, j] = jnp.zeros((18, 16, 256), BF)
    acc[...] = jnp.zeros_like(acc)

    pl.semaphore_wait(barrier, NX * 4 - 1 + NX + NY - 1 + 1)

    def spread(rows, dst, first):
        n = rows.shape[0]
        v = rows[...].astype(F32).reshape(64 * n, 128)
        up, down = next_column(v), prev_column(v)
        nothing = jnp.zeros_like(v)
        pieces = (
            (merge(up, v), merge(down, nothing)),
            (merge_high(up, v), merge_high(down, nothing)),
        )
        for half in range(2):
            for side in range(2):
                dst[half, first:first + n, 0:4, :, 128 * side:128 * side + 128] = (
                    pieces[half][side].astype(BF).reshape(n, 4, 16, 128))

    def transposed_conv(w):
        for a, b in sorted(TAPS, reverse=True):
            n = 2 + a
            left = g3n[:, 2 - b:4 - b, 2 - a:4, :, 0:192]
            tap = 3 * (3 * a + b)
            right = w[tap:tap + 3].reshape(192, 512)
            v = dot(left.reshape(64 * n, 192), right, ((1,), (0,)))
            v = v.reshape(2, 2, n, 16, 512)
            if (a, b) == (2, 2):
                part[...] = v
            else:
                part[:, :, 0:n] = part[:, :, 0:n] + v

    def scatter_begin(first, first_in):
        base = reserve("recv", 4)
        for i in range(4):
            low = part[0, :, :, :, 128 * i:128 * i + 128].reshape(128, 128)
            high = part[1, :, :, :, 128 * i:128 * i + 128].reshape(128, 128)
            even, odd = merge(low, high), merge_high(low, high)
            keep = jnp.where(c == 0, even, odd)
            give = jnp.where(c == 0, odd, even)
            own[i] = keep.reshape(2, 4, 16, 128)
            first[i] = give.astype(BF).reshape(2, 4, 16, 128)
            post(first.at[i], first_in.at[i], base + i, sibling)
        return base

    def scatter_on(base, first_in, second, second_in):
        after = reserve("recv", 4)
        for j in (2, 1, 3, 0):
            chip = (k + j) % 4
            await_into(first_in.at[chip], base + chip)
            v = own[chip] + first_in[chip].astype(F32)
            if j:
                second[chip] = v.astype(BF)
                post(second.at[chip], second_in.at[k], after + k, (d, h, 2 * chip + c))
            else:
                own[chip] = v
        return after

    def scatter_end(base, second_in):
        total = own[k]
        for j in range(1, 4):
            chip = (k + j) % 4
            await_into(second_in.at[chip], base + chip)
            total = total + second_in[chip].astype(F32)
        return total

    def near_begin(ref):
        base = reserve("recv", 2)
        post(ref.at[1], ref.at[3], base, (d, h - 1, t), h > 0)
        post(ref.at[2], ref.at[0], base + 1, (d, h + 1, t), h < NX * NZ - 1)
        return base

    def near_end(ref, base):
        @pl.when(h < NX * NZ - 1)
        def _():
            await_into(ref.at[3], base)

        @pl.when(h > 0)
        def _():
            await_into(ref.at[0], base + 1)

    def rows_of(ref, source):
        return ref.at[pl.ds(2 * source, 2)]

    def far_begin(ref):
        base = reserve("recv", 8)
        rows = rows_of(ref, h)
        post(rows, rows, base + h, (d, partner, t))
        for j in (1, 3, 2):
            post(rows, rows, base + h, (d, z * NX + (x + j) % NX, t))
        return base

    def far_relay(ref, base):
        rows = rows_of(ref, partner)
        await_into(rows, base + partner)
        for j in (1, 3, 2):
            post(rows, rows, base + partner, (d, z * NX + (x + j) % NX, t))

    def far_end(ref, base):
        for i in (z, 1 - z):
            for j in range(1, NX):
                other = i * NX + (x + j) % NX
                await_into(rows_of(ref, other), base + other)

    def transposed(packed):
        v = jnp.transpose(packed)
        return jnp.concatenate([v[:64], v[64:]], axis=1).astype(BF).reshape(4, 16, 256)

    def grad_begin(xt, g3, sf, sy, ry):
        base = reserve("recv", 12)
        for a in range(3):
            sides = []
            for b in range(3):
                total = None
                for s in range(NX * NZ):
                    left = xt[s // NX, s % NX].reshape(64, 256)
                    right = g3[:, 2 * s + 2 - b:2 * s + 4 - b, 2 - a:6 - a]
                    v = dot(left, right.reshape(256, 256), ((1,), (0,)))
                    total = v if total is None else total + v
                tile = total[:, 0:128].reshape(4, 16, 128)
                sf[:, a, b] = tile
                sy[:, a, b] = tile.astype(BF)
                sides.append(total[:, 128:256])
            for i, v in ((3, merge(sides[0], sides[1])), (4, sides[2])):
                tile = v.reshape(4, 16, 128)
                sf[:, a, i] = tile
                sy[:, a, i] = tile.astype(BF)
            for j in (2, 1, 3):
                other = (d + j) % NY
                post(sy.at[other, a], ry.at[d, a], base + 4 * a + d, (other, h, t))
        return base

    scale = 1.0 / math.sqrt(4 * 4 * 16 * 32)

    def grad_end(base, sf, ry, out):
        for a in range(3):
            v = sf[d, a]
            for j in range(1, NY):
                other = (d + j) % NY
                await_into(ry.at[other, a], base + 4 * a + other)
                v = v + ry[other, a].astype(F32)
            v = v * scale
            for b in range(3):
                tap = 9 * a + 3 * b
                out[tap] = v[b, :, 0:64]
                out[tap + 1] = v[b, :, 64:128]
                side = v[3 + b // 2]
                out[tap + 2] = side[:, 64:128] if b == 1 else side[:, 0:64]

    a_base = reserve("recv", 8)
    up_base = reserve("recv", 8)
    down_base = reserve("recv", 8)

    not_first, not_last = h > 0, h < NX * NZ - 1

    def halo(chip, up_when, down_when):
        post(xa.at[c, chip, 1], xa.at[c, chip, 3], up_base + 4 * c + chip,
             (d, h - 1, t), up_when)
        post(xa.at[c, chip, 2], xa.at[c, chip, 0], down_base + 4 * c + chip,
             (d, h + 1, t), down_when)

    mine = xa.at[c, k, pl.ds(1, 2)]
    for j in (2, 1, 3):
        post(mine, mine, a_base + 4 * c + k, (d, h, 2 * ((k + j) % 4) + c))
    post(mine, mine, a_base + 4 * c + k, sibling)
    cn_base = near_begin(cn)
    halo(k, not_first, not_last)

    near_end(cn, cn_base)
    spread(cn, g3n, 0)

    for j in (1, 3, 2):
        chip = (k + j) % 4
        rows = xa.at[c, chip, pl.ds(1, 2)]
        await_into(rows, a_base + 4 * c + chip)
        post(rows, rows, a_base + 4 * c + chip, sibling)
        halo(chip, not_first & (h != NX), not_last & (h != NX - 1))

    @pl.when(h == NX)
    def _():
        await_into(xa.at[c, k, 0], down_base + 4 * c + k)

    @pl.when(h == NX - 1)
    def _():
        await_into(xa.at[c, k, 3], up_base + 4 * c + k)

    for j in (2, 1, 3):
        peer = (d, h, 2 * ((k + j) % 4) + c)
        post(xa.at[c, k, 0], xa.at[c, k, 0], down_base + 4 * c + k, peer, h == NX)
        post(xa.at[c, k, 3], xa.at[c, k, 3], up_base + 4 * c + k, peer, h == NX - 1)

    for i in range(4):
        xs1[:, i] = transposed(xa[c, i, 1:3].astype(F32).reshape(128, 128))
    x1_base = reserve("recv", 8)
    for j in (2, 1, 3, 0):
        other = (x + j) % NX
        post(xs1.at[other], xt1.at[z, x], x1_base + h, (d, c * NX + other, t),
             None if j else jnp.logical_not(home))

    @pl.when(home)
    def _():
        xt1[z, x] = xs1[x]

    copies[3].wait()
    transposed_conv(w2)
    e_base = scatter_begin(e1, e1r)
    c_base = far_begin(gc)

    for row, base, when, edge in (
        (3, up_base, not_last, NX - 1), (0, down_base, not_first, NX)
    ):
        for j in range(4):
            chip = (k + j) % 4

            @pl.when(when if j else when & (h != edge))
            def _():
                await_into(xa.at[c, chip, row], base + 4 * c + chip)

    up_sib = reserve("recv", 1)
    post(xa.at[c, :, 3], xa.at[c, :, 3], up_sib, sibling, not_last)
    down_sib = reserve("recv", 1)
    post(xa.at[c, :, 0], xa.at[c, :, 0], down_sib, sibling, not_first)

    e_base = scatter_on(e_base, e1r, e2, e2r)

    for j in range(4):
        chip = (k + j) % 4
        await_into(xa.at[1 - c, chip, pl.ds(1, 2)], a_base + 4 * (1 - c) + chip)

    @pl.when(not_last)
    def _():
        await_into(xa.at[1 - c, :, 3], up_sib)

    @pl.when(not_first)
    def _():
        await_into(xa.at[1 - c, :, 0], down_sib)

    for i in range(4):
        first = xa[0, i].astype(F32).reshape(256, 128)
        second = xa[1, i].astype(F32).reshape(256, 128)
        xn[0, :, :, :, 128 * i:128 * i + 128] = (
            merge(first, second).astype(BF).reshape(4, 4, 16, 128))
        xn[1, :, :, :, 128 * i:128 * i + 128] = (
            merge_high(first, second).astype(BF).reshape(4, 4, 16, 128))

    copies[4].wait()
    for a, b in TAPS:
        n = 2 + a
        left = xn[:, b:b + 2, 0:n].reshape(64 * n, 512)
        tap = 3 * (3 * a + b)
        right = w1[tap:tap + 3].reshape(192, 512)
        v = dot(left, right, ((1,), (1,))).reshape(2, 2, n, 16, 192)
        acc[:, :, 2 - a:4, :, 0:192] = acc[:, :, 2 - a:4, :, 0:192] + v
    low0 = acc[0, :, :, :, 0:128].reshape(128, 128)
    low1 = acc[0, :, :, :, 128:256].reshape(128, 128)
    high0 = acc[1, :, :, :, 0:128].reshape(128, 128)
    high1 = acc[1, :, :, :, 128:256].reshape(128, 128)
    wide_bias = jnp.concatenate([bias[...], bias[...]], axis=1)
    preact = (prev_column(merge(low0, high0)) + merge_high(low0, high0)
              + next_column(merge(low1, high1)) + wide_bias)
    act_two = silu(preact).astype(BF).astype(F32)

    xs2[...] = transposed(act_two)
    x2_cross = reserve("recv", 1)
    x2_base = reserve("recv", 32)
    post(xs2, xr2, x2_cross, (d, partner, t), jnp.logical_not(home))

    def distribute(src, half):
        for i in (0, 1, 3, 2):
            for j in (2, 1, 3, 0):
                if i or j:
                    other, chip = (x + i) % NX, (k + j) % 4
                    post(src.at[other], xt2.at[half, x, k],
                         x2_base + 16 * half + 4 * x + k,
                         (d, z * NX + other, 2 * chip + c), home)

        @pl.when(home)
        def _():
            xt2[half, x, k] = src[x]

    distribute(xs2, z)
    far_relay(gc, c_base)

    grad_pre = scatter_end(e_base, e2r).reshape(128, 128) * slope(preact)
    grad_rows = grad_pre.astype(BF).reshape(2, 4, 16, 128)
    gn[1:3] = grad_rows
    gp[pl.ds(2 * h, 2)] = grad_rows
    gn_base = near_begin(gn)
    p_base = far_begin(gp)

    @pl.when(home)
    def _():
        await_into(xr2, x2_cross)

    distribute(xr2, 1 - z)

    x1_sib = reserve("recv", 8)
    for i in (z, 1 - z):
        for j in range(NX):
            other = (x + j) % NX
            block = xt1.at[i, other]
            source = i * NX + other

            @pl.when(home if j else home & (i != z))
            def _():
                await_into(block, x1_base + source)

            post(block, block, x1_sib + source, sibling, home)

    far_end(gc, c_base)
    spread(gc, g3c, 1)

    near_end(gn, gn_base)
    spread(gn, g3n, 0)
    transposed_conv(w1)
    h_base = scatter_begin(h1, h1r)
    far_relay(gp, p_base)

    x2_sib = reserve("recv", 8)
    for half in (z, 1 - z):
        for i in range(NX):
            other = (x + i) % NX

            @pl.when(home)
            def _():
                for j in range(4):
                    chip = (k + j) % 4
                    if i or j:
                        await_into(xt2.at[half, other, chip],
                                   x2_base + 16 * half + 4 * other + chip)

            post(xt2.at[half, other], xt2.at[half, other],
                 x2_sib + NX * half + other, sibling, home)

    h_base = scatter_on(h_base, h1r, h2, h2r)

    def await_sibling(xt, base):
        @pl.when(jnp.logical_not(home))
        def _():
            for i in range(NX * NZ):
                await_into(xt.at[i // NX, i % NX], base + i)

    await_sibling(xt2, x2_sib)
    y2_base = grad_begin(xt2, g3c, sf2, sy2, ry2)
    far_end(gp, p_base)
    spread(gp, g3p, 1)
    await_sibling(xt1, x1_sib)
    y1_base = grad_begin(xt1, g3p, sf1, sy1, ry1)

    back = scatter_end(h_base, h2r)
    grad_in = cotp[...] + back * slope(featp[...])
    for r in range(2):
        for f in range(4):
            out_in[0, f, r, 0:16] = grad_in[r, f, :, 0:64].astype(BF)
            out_in[0, f, r, 16:32] = grad_in[r, f, :, 64:128].astype(BF)
    results = [
        pltpu.make_async_copy(src, dst, out_sem.at[i]) for i, (src, dst) in enumerate(
            [(out_in, in_hbm), (out_two, two_hbm), (out_one, one_hbm)])
    ]
    results[0].start()
    grad_end(y2_base, sf2, ry2, out_two)
    results[1].start()
    grad_end(y1_base, sf1, ry1, out_one)
    results[2].start()

    for finish, when in unfinished:
        if when is None:
            finish()
        else:
            pl.when(when)(finish)
    for copy in results:
        copy.wait()
    assert counts["send"] <= SENDS and counts["recv"] <= RECVS


def write_kernel(a, b, c, a_out, b_out, c_out, a_mid, b_mid, c_mid, in_sem, out_sem):
    stages = [(a, a_mid, a_out), (b, b_mid, b_out), (c, c_mid, c_out)]
    first = [
        pltpu.make_async_copy(src, mid, in_sem.at[i])
        for i, (src, mid, _) in enumerate(stages)
    ]
    second = [
        pltpu.make_async_copy(mid, dst, out_sem.at[i])
        for i, (_, mid, dst) in enumerate(stages)
    ]
    for copy in first:
        copy.start()
    for copy, after in zip(first, second):
        copy.wait()
        after.start()
    for copy in second:
        copy.wait()


def local(features, cotangent, conv_one, bias_one, conv_two):
    hbm = pl.BlockSpec(memory_space=pltpu.HBM)
    grad_in_shape = (1, 4, 2, 32, 64)
    block = (2, 4, 16, 128)
    blocks = pltpu.VMEM((4,) + block, BF)
    near = pltpu.VMEM((4, 4, 16, 128), BF)
    far = pltpu.VMEM((16, 4, 16, 128), BF)
    wide = pltpu.VMEM((2, 18, 6, 16, 256), BF)
    turned = pltpu.VMEM((4, 16, 256), BF)
    clip = pltpu.VMEM((2, 4, 4, 16, 256), BF)
    sums = pltpu.VMEM((4, 3, 5, 16, 128), F32)
    sent = pltpu.VMEM((4, 3, 5, 16, 128), BF)
    kernel_block = pltpu.VMEM((27, 64, 512), BF)
    scratch = [
        pltpu.VMEM(grad_in_shape, BF), pltpu.VMEM(grad_in_shape, BF),
        pltpu.VMEM((1, 64), F32), kernel_block, kernel_block,
        pltpu.VMEM((2, 4, 4, 4, 16, 128), BF), pltpu.VMEM((2, 4, 4, 16, 512), BF),
        near, near, far, far, pltpu.VMEM((2, 4, 4, 16, 256), BF), wide, wide,
        pltpu.VMEM((2, 2, 4, 16, 512), F32), pltpu.VMEM((2, 2, 4, 16, 256), F32),
        pltpu.VMEM((4,) + block, F32),
        blocks, blocks, blocks, blocks, blocks, blocks, blocks, blocks,
        pltpu.VMEM((4, 4, 16, 256), BF), turned, turned, clip, clip,
        sums, sums, sent, sent, sent, sent,
        pltpu.VMEM(block, F32), pltpu.VMEM(block, F32),
        pltpu.VMEM(grad_in_shape, BF),
        pltpu.VMEM((27, 16, 64), F32), pltpu.VMEM((27, 16, 64), F32),
        pltpu.SemaphoreType.DMA((5,)), pltpu.SemaphoreType.DMA((3,)),
        pltpu.SemaphoreType.DMA((SENDS,)), pltpu.SemaphoreType.DMA((RECVS,)),
    ]
    out_shape = (
        jax.ShapeDtypeStruct(grad_in_shape, BF),
        jax.ShapeDtypeStruct((27, 16, 64), F32),
        jax.ShapeDtypeStruct((27, 16, 64), F32),
    )
    outs = pl.pallas_call(
        kernel,
        out_shape=out_shape,
        in_specs=[hbm, hbm, hbm, hbm, hbm],
        out_specs=(hbm, hbm, hbm),
        scratch_shapes=scratch,
        compiler_params=pltpu.CompilerParams(
            collective_id=0, has_side_effects=True, vmem_limit_bytes=56 * 1024 * 1024
        ),
    )(features, cotangent, bias_one.reshape(1, -1), conv_one, conv_two)
    return pl.pallas_call(
        write_kernel,
        out_shape=out_shape,
        in_specs=[hbm, hbm, hbm],
        out_specs=(hbm, hbm, hbm),
        scratch_shapes=[
            pltpu.VMEM(grad_in_shape, BF),
            pltpu.VMEM((27, 16, 64), F32), pltpu.VMEM((27, 16, 64), F32),
            pltpu.SemaphoreType.DMA((3,)), pltpu.SemaphoreType.DMA((3,)),
        ],
        compiler_params=pltpu.CompilerParams(vmem_limit_bytes=60 * 1024 * 1024),
    )(*outs)


def solution(mesh):
    in_specs = (
        P("dp", None, "height", None, "tensor"),
        P("dp", None, "height", None, "tensor"),
        P(None, "tensor", None),
        P("tensor"),
        P(None, "tensor", None),
    )
    out_specs = (
        P("dp", None, "height", None, "tensor"),
        P(None, ("dp", "height"), "tensor"),
        P(None, ("dp", "height"), "tensor"),
    )
    return jax.shard_map(local, mesh=mesh, in_specs=in_specs, out_specs=out_specs, check_vma=False)
```

```python
import math

import jax
import jax.numpy as jnp
from jax import lax
from jax.experimental import pallas as pl
from jax.experimental.pallas import tpu as pltpu
from jax.sharding import PartitionSpec as P

BF = jnp.bfloat16
F32 = jnp.float32
MESH = pl.DeviceIdType.MESH

NX, NZ, NY, NT = 4, 2, 4, 8
SENDS, RECVS = 136, 160
TAPS = [(a, b) for a in range(3) for b in range(3)]


def iota(shape, dim):
    return lax.broadcasted_iota(jnp.int32, shape, dim)


def swap(v):
    return pltpu.roll(v, 64, 1)


def low_lane(v):
    return iota(v.shape, 1) < 64


def next_column(v):
    rows = v.shape[0]
    edge = jnp.where(low_lane(v), swap(pltpu.roll(v, 15, 0)), 0.0)
    return jnp.where(iota(v.shape, 0) % 16 == 15, edge, pltpu.roll(v, rows - 1, 0))


def prev_column(v):
    rows = v.shape[0]
    edge = jnp.where(low_lane(v), 0.0, swap(pltpu.roll(v, rows - 15, 0)))
    return jnp.where(iota(v.shape, 0) % 16 == 0, edge, pltpu.roll(v, 1, 0))


def merge(first, second):
    return jnp.where(low_lane(first), first, swap(second))


def merge_high(first, second):
    return jnp.where(low_lane(first), swap(first), second)


def slope(v):
    sig = jax.nn.sigmoid(v)
    return sig * (1.0 + v * (1.0 - sig))


def silu(v):
    return v * jax.nn.sigmoid(v)


def dot(left, right, dims):
    return lax.dot_general(left, right, (dims, ((), ())), preferred_element_type=F32)


def kernel(
    feat_hbm, cot_hbm, bias_hbm, w1_hbm, w2_hbm,
    in_hbm, one_hbm, two_hbm,
    feat, cot, bias, w1, w2, xa, xn, cn, gn, gc, gp, g3n, g3c, g3p, part, acc,
    own, e1, e1r, e2, e2r, h1, h1r, h2, h2r,
    xs1, xs2, xr2, xt1, xt2, sf1, sf2, sy1, sy2, ry1, ry2,
    featp, cotp, out_in, out_one, out_two, in_sem, out_sem, send_sem, recv_sem,
):
    d = lax.axis_index("dp")
    h = lax.axis_index("height")
    t = lax.axis_index("tensor")
    x = h % NX
    z = h // NX
    k = t // 2
    c = t % 2
    home = c == z
    partner = (1 - z) * NX + x
    here = (d, h, t)
    sibling = (d, h, 2 * k + 1 - c)

    copies = [
        pltpu.make_async_copy(src, dst, in_sem.at[i]) for i, (src, dst) in enumerate(
            [(feat_hbm, feat), (cot_hbm, cot), (bias_hbm, bias), (w2_hbm, w2), (w1_hbm, w1)])
    ]
    for copy in copies:
        copy.start()

    counts = {"send": 0, "recv": 0}

    def reserve(kind, n):
        base = counts[kind]
        counts[kind] = base + n
        return base

    def remote(src, dst, s, r, where):
        return pltpu.make_async_remote_copy(
            src_ref=src, dst_ref=dst, send_sem=send_sem.at[s], recv_sem=recv_sem.at[r],
            device_id=where, device_id_type=MESH,
        )

    unfinished = []

    def post(src, dst, r, where, when=None):
        s = reserve("send", 1)

        def make():
            return remote(src, dst, s, r, where)

        def begin():
            make().start()

        def finish():
            make().wait_send()

        if when is None:
            begin()
        else:
            pl.when(when)(begin)
        unfinished.append((finish, when))

    def finish_all():
        for finish, when in unfinished:
            if when is None:
                finish()
            else:
                pl.when(when)(finish)
        unfinished.clear()

    def await_into(dst, r):
        remote(dst, dst, 0, r, here).wait_recv()

    barrier = pltpu.get_barrier_semaphore()

    def greet(where):
        pl.semaphore_signal(barrier, inc=1, device_id=where, device_id_type=MESH)

    for i in range(NX):
        for j in range(4):
            if i or j:
                greet((d, z * NX + (x + i) % NX, 2 * ((k + j) % 4) + c))
        greet((d, (1 - z) * NX + i, t))
    for i in range(1, NY):
        greet(((d + i) % NY, h, t))
    greet(sibling)

    copies[0].wait()
    copies[1].wait()
    copies[2].wait()
    for r in range(2):
        for f in range(4):
            v = feat[0, f, r].astype(F32)
            v = jnp.concatenate([v[:16], v[16:]], axis=-1)
            featp[r, f] = v
            xa[c, k, 1 + r, f] = silu(v).astype(BF)
            v = cot[0, f, r].astype(F32)
            v = jnp.concatenate([v[:16], v[16:]], axis=-1)
            cotp[r, f] = v
            cn[1 + r, f] = v.astype(BF)
            gc[2 * h + r, f] = v.astype(BF)

    zero_row = jnp.zeros((4, 16, 128), BF)
    @pl.when(h == 0)
    def _():
        for i in range(2):
            for j in range(4):
                xa[i, j, 0] = zero_row
        cn[0] = zero_row
        gn[0] = zero_row

    @pl.when(h == NX * NZ - 1)
    def _():
        for i in range(2):
            for j in range(4):
                xa[i, j, 3] = zero_row
        cn[3] = zero_row
        gn[3] = zero_row

    for ref in (g3c, g3p):
        for i in range(2):
            for j in (0, 17):
                ref[i, j] = jnp.zeros((6, 16, 256), BF)
            for j in (4, 5):
                ref[i, :, j] = jnp.zeros((18, 16, 256), BF)
    acc[...] = jnp.zeros_like(acc)

    pl.semaphore_wait(barrier, NX * 4 - 1 + NX + NY - 1 + 1)

    def spread(rows, dst, first):
        n = rows.shape[0]
        v = rows[...].astype(F32).reshape(64 * n, 128)
        up, down = next_column(v), prev_column(v)
        nothing = jnp.zeros_like(v)
        pieces = (
            (merge(up, v), merge(down, nothing)),
            (merge_high(up, v), merge_high(down, nothing)),
        )
        for half in range(2):
            for side in range(2):
                dst[half, first:first + n, 0:4, :, 128 * side:128 * side + 128] = (
                    pieces[half][side].astype(BF).reshape(n, 4, 16, 128))

    def transposed_conv(w):
        for a, b in sorted(TAPS, reverse=True):
            n = 2 + a
            left = g3n[:, 2 - b:4 - b, 2 - a:4, :, 0:192]
            tap = 3 * (3 * a + b)
            right = w[tap:tap + 3].reshape(192, 512)
            v = dot(left.reshape(64 * n, 192), right, ((1,), (0,)))
            v = v.reshape(2, 2, n, 16, 512)
            if (a, b) == (2, 2):
                part[...] = v
            else:
                part[:, :, 0:n] = part[:, :, 0:n] + v

    def scatter_begin(first, first_in):
        base = reserve("recv", 4)
        for i in range(4):
            low = part[0, :, :, :, 128 * i:128 * i + 128].reshape(128, 128)
            high = part[1, :, :, :, 128 * i:128 * i + 128].reshape(128, 128)
            even, odd = merge(low, high), merge_high(low, high)
            keep = jnp.where(c == 0, even, odd)
            give = jnp.where(c == 0, odd, even)
            own[i] = keep.reshape(2, 4, 16, 128)
            first[i] = give.astype(BF).reshape(2, 4, 16, 128)
            post(first.at[i], first_in.at[i], base + i, sibling)
        return base

    def scatter_on(base, first_in, second, second_in):
        after = reserve("recv", 4)
        for j in (2, 1, 3, 0):
            chip = (k + j) % 4
            await_into(first_in.at[chip], base + chip)
            v = own[chip] + first_in[chip].astype(F32)
            if j:
                second[chip] = v.astype(BF)
                post(second.at[chip], second_in.at[k], after + k, (d, h, 2 * chip + c))
            else:
                own[chip] = v
        return after

    def scatter_end(base, second_in):
        total = own[k]
        for j in range(1, 4):
            chip = (k + j) % 4
            await_into(second_in.at[chip], base + chip)
            total = total + second_in[chip].astype(F32)
        return total

    def near_begin(ref):
        base = reserve("recv", 2)
        post(ref.at[1], ref.at[3], base, (d, h - 1, t), h > 0)
        post(ref.at[2], ref.at[0], base + 1, (d, h + 1, t), h < NX * NZ - 1)
        return base

    def near_end(ref, base):
        @pl.when(h < NX * NZ - 1)
        def _():
            await_into(ref.at[3], base)

        @pl.when(h > 0)
        def _():
            await_into(ref.at[0], base + 1)

    def rows_of(ref, source):
        return ref.at[pl.ds(2 * source, 2)]

    def far_begin(ref):
        base = reserve("recv", 8)
        rows = rows_of(ref, h)
        post(rows, rows, base + h, (d, partner, t))
        for j in (1, 3, 2):
            post(rows, rows, base + h, (d, z * NX + (x + j) % NX, t))
        return base

    def far_relay(ref, base):
        rows = rows_of(ref, partner)
        await_into(rows, base + partner)
        for j in (1, 3, 2):
            post(rows, rows, base + partner, (d, z * NX + (x + j) % NX, t))

    def far_end(ref, base):
        for i in (z, 1 - z):
            for j in range(1, NX):
                other = i * NX + (x + j) % NX
                await_into(rows_of(ref, other), base + other)

    def transposed(packed):
        v = jnp.transpose(packed)
        return jnp.concatenate([v[:64], v[64:]], axis=1).astype(BF).reshape(4, 16, 256)

    def grad_begin(xt, g3, sf, sy, ry, parts):
        base = reserve("recv", 12)
        for a in range(3):
            sides = []
            for b in range(3):
                total = None
                for s in range(NX * NZ):
                    left = xt[s // NX, s % NX].reshape(64, 256)
                    right = g3[:, 2 * s + 2 - b:2 * s + 4 - b, 2 - a:6 - a]
                    v = dot(left, right.reshape(256, 256), ((1,), (0,)))
                    total = v if total is None else total + v
                tile = total[:, 0:128].reshape(4, 16, 128)
                sf[:, a, b] = tile
                sy[:, a, b] = tile.astype(BF)
                sides.append(total[:, 128:256])
            for i, v in ((3, merge(sides[0], sides[1])), (4, sides[2])):
                tile = v.reshape(4, 16, 128)
                sf[:, a, i] = tile
                sy[:, a, i] = tile.astype(BF)
            for first, n in parts:
                if first + n - 1 == a:
                    piece = pl.ds(first, n)
                    for j in (2, 1, 3):
                        other = (d + j) % NY
                        post(sy.at[other, piece], ry.at[d, piece], base + 4 * first + d,
                             (other, h, t))
        return base

    scale = 1.0 / math.sqrt(4 * 4 * 16 * 32)

    def grad_end(base, sf, ry, out, parts):
        for first, n in parts:
            v = sf[d, first:first + n]
            for j in range(1, NY):
                other = (d + j) % NY
                await_into(ry.at[other, pl.ds(first, n)], base + 4 * first + other)
                v = v + ry[other, first:first + n].astype(F32)
            v = v * scale
            for a in range(n):
                for b in range(3):
                    tap = 9 * (first + a) + 3 * b
                    out[tap] = v[a, b, :, 0:64]
                    out[tap + 1] = v[a, b, :, 64:128]
                    side = v[a, 3 + b // 2]
                    out[tap + 2] = side[:, 64:128] if b == 1 else side[:, 0:64]

    a_base = reserve("recv", 8)
    up_base = reserve("recv", 8)
    down_base = reserve("recv", 8)

    not_first, not_last = h > 0, h < NX * NZ - 1

    def halo(chip, up_when, down_when):
        post(xa.at[c, chip, 1], xa.at[c, chip, 3], up_base + 4 * c + chip,
             (d, h - 1, t), up_when)
        post(xa.at[c, chip, 2], xa.at[c, chip, 0], down_base + 4 * c + chip,
             (d, h + 1, t), down_when)

    mine = xa.at[c, k, pl.ds(1, 2)]
    for j in (2, 1, 3):
        post(mine, mine, a_base + 4 * c + k, (d, h, 2 * ((k + j) % 4) + c))
    post(mine, mine, a_base + 4 * c + k, sibling)
    cn_base = near_begin(cn)
    halo(k, not_first, not_last)

    near_end(cn, cn_base)
    spread(cn, g3n, 0)

    for j in (1, 3, 2):
        chip = (k + j) % 4
        rows = xa.at[c, chip, pl.ds(1, 2)]
        await_into(rows, a_base + 4 * c + chip)
        post(rows, rows, a_base + 4 * c + chip, sibling)
        halo(chip, not_first & (h != NX), not_last & (h != NX - 1))

    @pl.when(h == NX)
    def _():
        await_into(xa.at[c, k, 0], down_base + 4 * c + k)

    @pl.when(h == NX - 1)
    def _():
        await_into(xa.at[c, k, 3], up_base + 4 * c + k)

    for j in (2, 1, 3):
        peer = (d, h, 2 * ((k + j) % 4) + c)
        post(xa.at[c, k, 0], xa.at[c, k, 0], down_base + 4 * c + k, peer, h == NX)
        post(xa.at[c, k, 3], xa.at[c, k, 3], up_base + 4 * c + k, peer, h == NX - 1)

    for i in range(4):
        xs1[:, i] = transposed(xa[c, i, 1:3].astype(F32).reshape(128, 128))
    x1_base = reserve("recv", 8)

    @pl.when(home)
    def _():
        xt1[z, x] = xs1[x]

    copies[3].wait()
    transposed_conv(w2)
    e_base = scatter_begin(e1, e1r)
    c_base = far_begin(gc)

    for row, base, when, edge in (
        (3, up_base, not_last, NX - 1), (0, down_base, not_first, NX)
    ):
        for j in range(4):
            chip = (k + j) % 4

            @pl.when(when if j else when & (h != edge))
            def _():
                await_into(xa.at[c, chip, row], base + 4 * c + chip)

    up_sib = reserve("recv", 1)
    post(xa.at[c, :, 3], xa.at[c, :, 3], up_sib, sibling, not_last)
    down_sib = reserve("recv", 1)
    post(xa.at[c, :, 0], xa.at[c, :, 0], down_sib, sibling, not_first)

    e_base = scatter_on(e_base, e1r, e2, e2r)

    for j in range(4):
        chip = (k + j) % 4
        await_into(xa.at[1 - c, chip, pl.ds(1, 2)], a_base + 4 * (1 - c) + chip)

    @pl.when(not_last)
    def _():
        await_into(xa.at[1 - c, :, 3], up_sib)

    @pl.when(not_first)
    def _():
        await_into(xa.at[1 - c, :, 0], down_sib)

    for i in range(4):
        first = xa[0, i].astype(F32).reshape(256, 128)
        second = xa[1, i].astype(F32).reshape(256, 128)
        xn[0, :, :, :, 128 * i:128 * i + 128] = (
            merge(first, second).astype(BF).reshape(4, 4, 16, 128))
        xn[1, :, :, :, 128 * i:128 * i + 128] = (
            merge_high(first, second).astype(BF).reshape(4, 4, 16, 128))

    copies[4].wait()
    for a, b in TAPS:
        n = 2 + a
        left = xn[:, b:b + 2, 0:n].reshape(64 * n, 512)
        tap = 3 * (3 * a + b)
        right = w1[tap:tap + 3].reshape(192, 512)
        v = dot(left, right, ((1,), (1,))).reshape(2, 2, n, 16, 192)
        acc[:, :, 2 - a:4, :, 0:192] = acc[:, :, 2 - a:4, :, 0:192] + v
    low0 = acc[0, :, :, :, 0:128].reshape(128, 128)
    low1 = acc[0, :, :, :, 128:256].reshape(128, 128)
    high0 = acc[1, :, :, :, 0:128].reshape(128, 128)
    high1 = acc[1, :, :, :, 128:256].reshape(128, 128)
    wide_bias = jnp.concatenate([bias[...], bias[...]], axis=1)
    preact = (prev_column(merge(low0, high0)) + merge_high(low0, high0)
              + next_column(merge(low1, high1)) + wide_bias)
    act_two = silu(preact).astype(BF).astype(F32)

    xs2[...] = transposed(act_two)
    x2_cross = reserve("recv", 1)
    x2_base = reserve("recv", 32)
    post(xs2, xr2, x2_cross, (d, partner, t), jnp.logical_not(home))

    def distribute(src, half):
        for i in (0, 1, 3, 2):
            for j in (2, 1, 3, 0):
                if i or j:
                    other, chip = (x + i) % NX, (k + j) % 4
                    post(src.at[other], xt2.at[half, x, k],
                         x2_base + 16 * half + 4 * x + k,
                         (d, z * NX + other, 2 * chip + c), home)

        @pl.when(home)
        def _():
            xt2[half, x, k] = src[x]

    distribute(xs2, z)
    for j in (2, 1, 3, 0):
        other = (x + j) % NX
        post(xs1.at[other], xt1.at[z, x], x1_base + h, (d, c * NX + other, t),
             None if j else jnp.logical_not(home))
    far_relay(gc, c_base)

    grad_pre = scatter_end(e_base, e2r).reshape(128, 128) * slope(preact)
    grad_rows = grad_pre.astype(BF).reshape(2, 4, 16, 128)
    gn[1:3] = grad_rows
    gp[pl.ds(2 * h, 2)] = grad_rows
    gn_base = near_begin(gn)
    p_base = far_begin(gp)

    @pl.when(home)
    def _():
        await_into(xr2, x2_cross)

    distribute(xr2, 1 - z)

    x1_sib = reserve("recv", 8)
    for i in (z, 1 - z):
        for j in range(NX):
            other = (x + j) % NX
            block = xt1.at[i, other]
            source = i * NX + other

            @pl.when(home if j else home & (i != z))
            def _():
                await_into(block, x1_base + source)

        post(xt1.at[i], xt1.at[i], x1_sib + i, sibling, home)

    far_end(gc, c_base)
    spread(gc, g3c, 1)

    near_end(gn, gn_base)
    spread(gn, g3n, 0)
    transposed_conv(w1)
    h_base = scatter_begin(h1, h1r)
    far_relay(gp, p_base)

    x2_sib = reserve("recv", 8)
    for half in (z, 1 - z):
        for i in range(NX):
            other = (x + i) % NX

            @pl.when(home)
            def _():
                for j in range(4):
                    chip = (k + j) % 4
                    if i or j:
                        await_into(xt2.at[half, other, chip],
                                   x2_base + 16 * half + 4 * other + chip)

        post(xt2.at[half], xt2.at[half], x2_sib + half, sibling, home)

    h_base = scatter_on(h_base, h1r, h2, h2r)

    def await_sibling(xt, base):
        @pl.when(jnp.logical_not(home))
        def _():
            for i in range(NZ):
                await_into(xt.at[i], base + i)

    whole, cut = ((0, 3),), ((0, 1), (1, 1), (2, 1))
    await_sibling(xt2, x2_sib)
    y2_base = grad_begin(xt2, g3c, sf2, sy2, ry2, whole)
    far_end(gp, p_base)
    spread(gp, g3p, 1)
    await_sibling(xt1, x1_sib)
    y1_base = grad_begin(xt1, g3p, sf1, sy1, ry1, cut)
    finish_all()

    back = scatter_end(h_base, h2r)
    grad_in = cotp[...] + back * slope(featp[...])
    for r in range(2):
        for f in range(4):
            out_in[0, f, r, 0:16] = grad_in[r, f, :, 0:64].astype(BF)
            out_in[0, f, r, 16:32] = grad_in[r, f, :, 64:128].astype(BF)
    results = [
        pltpu.make_async_copy(src, dst, out_sem.at[i]) for i, (src, dst) in enumerate(
            [(out_in, in_hbm), (out_two, two_hbm), (out_one, one_hbm)])
    ]
    results[0].start()
    grad_end(y2_base, sf2, ry2, out_two, whole)
    results[1].start()
    grad_end(y1_base, sf1, ry1, out_one, cut)
    results[2].start()

    finish_all()
    for copy in results:
        copy.wait()
    assert counts["send"] <= SENDS and counts["recv"] <= RECVS


def write_kernel(a, b, c, a_out, b_out, c_out, a_mid, b_mid, c_mid, in_sem, out_sem):
    stages = [(a, a_mid, a_out), (b, b_mid, b_out), (c, c_mid, c_out)]
    first = [
        pltpu.make_async_copy(src, mid, in_sem.at[i])
        for i, (src, mid, _) in enumerate(stages)
    ]
    second = [
        pltpu.make_async_copy(mid, dst, out_sem.at[i])
        for i, (_, mid, dst) in enumerate(stages)
    ]
    for copy in first:
        copy.start()
    for copy, after in zip(first, second):
        copy.wait()
        after.start()
    for copy in second:
        copy.wait()


def local(features, cotangent, conv_one, bias_one, conv_two):
    hbm = pl.BlockSpec(memory_space=pltpu.HBM)
    grad_in_shape = (1, 4, 2, 32, 64)
    block = (2, 4, 16, 128)
    blocks = pltpu.VMEM((4,) + block, BF)
    near = pltpu.VMEM((4, 4, 16, 128), BF)
    far = pltpu.VMEM((16, 4, 16, 128), BF)
    wide = pltpu.VMEM((2, 18, 6, 16, 256), BF)
    turned = pltpu.VMEM((4, 16, 256), BF)
    clip = pltpu.VMEM((2, 4, 4, 16, 256), BF)
    sums = pltpu.VMEM((4, 3, 5, 16, 128), F32)
    sent = pltpu.VMEM((4, 3, 5, 16, 128), BF)
    kernel_block = pltpu.VMEM((27, 64, 512), BF)
    scratch = [
        pltpu.VMEM(grad_in_shape, BF), pltpu.VMEM(grad_in_shape, BF),
        pltpu.VMEM((1, 64), F32), kernel_block, kernel_block,
        pltpu.VMEM((2, 4, 4, 4, 16, 128), BF), pltpu.VMEM((2, 4, 4, 16, 512), BF),
        near, near, far, far, pltpu.VMEM((2, 4, 4, 16, 256), BF), wide, wide,
        pltpu.VMEM((2, 2, 4, 16, 512), F32), pltpu.VMEM((2, 2, 4, 16, 256), F32),
        pltpu.VMEM((4,) + block, F32),
        blocks, blocks, blocks, blocks, blocks, blocks, blocks, blocks,
        pltpu.VMEM((4, 4, 16, 256), BF), turned, turned, clip, clip,
        sums, sums, sent, sent, sent, sent,
        pltpu.VMEM(block, F32), pltpu.VMEM(block, F32),
        pltpu.VMEM(grad_in_shape, BF),
        pltpu.VMEM((27, 16, 64), F32), pltpu.VMEM((27, 16, 64), F32),
        pltpu.SemaphoreType.DMA((5,)), pltpu.SemaphoreType.DMA((3,)),
        pltpu.SemaphoreType.DMA((SENDS,)), pltpu.SemaphoreType.DMA((RECVS,)),
    ]
    out_shape = (
        jax.ShapeDtypeStruct(grad_in_shape, BF),
        jax.ShapeDtypeStruct((27, 16, 64), F32),
        jax.ShapeDtypeStruct((27, 16, 64), F32),
    )
    outs = pl.pallas_call(
        kernel,
        out_shape=out_shape,
        in_specs=[hbm, hbm, hbm, hbm, hbm],
        out_specs=(hbm, hbm, hbm),
        scratch_shapes=scratch,
        compiler_params=pltpu.CompilerParams(
            collective_id=0, has_side_effects=True, vmem_limit_bytes=56 * 1024 * 1024
        ),
    )(features, cotangent, bias_one.reshape(1, -1), conv_one, conv_two)
    return pl.pallas_call(
        write_kernel,
        out_shape=out_shape,
        in_specs=[hbm, hbm, hbm],
        out_specs=(hbm, hbm, hbm),
        scratch_shapes=[
            pltpu.VMEM(grad_in_shape, BF),
            pltpu.VMEM((27, 16, 64), F32), pltpu.VMEM((27, 16, 64), F32),
            pltpu.SemaphoreType.DMA((3,)), pltpu.SemaphoreType.DMA((3,)),
        ],
        compiler_params=pltpu.CompilerParams(vmem_limit_bytes=60 * 1024 * 1024),
    )(*outs)


def solution(mesh):
    in_specs = (
        P("dp", None, "height", None, "tensor"),
        P("dp", None, "height", None, "tensor"),
        P(None, "tensor", None),
        P("tensor"),
        P(None, "tensor", None),
    )
    out_specs = (
        P("dp", None, "height", None, "tensor"),
        P(None, ("dp", "height"), "tensor"),
        P(None, ("dp", "height"), "tensor"),
    )
    return jax.shard_map(local, mesh=mesh, in_specs=in_specs, out_specs=out_specs, check_vma=False)
```

```python
import math

import jax
import jax.numpy as jnp
from jax import lax
from jax.experimental import pallas as pl
from jax.experimental.pallas import tpu as pltpu
from jax.sharding import PartitionSpec as P

BF = jnp.bfloat16
F32 = jnp.float32
MESH = pl.DeviceIdType.MESH

NX, NZ, NY, NT = 4, 2, 4, 8
SENDS, RECVS = 136, 160
TAPS = [(a, b) for a in range(3) for b in range(3)]


def iota(shape, dim):
    return lax.broadcasted_iota(jnp.int32, shape, dim)


def swap(v):
    return pltpu.roll(v, 64, 1)


def low_lane(v):
    return iota(v.shape, 1) < 64


def next_column(v):
    rows = v.shape[0]
    edge = jnp.where(low_lane(v), swap(pltpu.roll(v, 15, 0)), 0.0)
    return jnp.where(iota(v.shape, 0) % 16 == 15, edge, pltpu.roll(v, rows - 1, 0))


def prev_column(v):
    rows = v.shape[0]
    edge = jnp.where(low_lane(v), 0.0, swap(pltpu.roll(v, rows - 15, 0)))
    return jnp.where(iota(v.shape, 0) % 16 == 0, edge, pltpu.roll(v, 1, 0))


def merge(first, second):
    return jnp.where(low_lane(first), first, swap(second))


def merge_high(first, second):
    return jnp.where(low_lane(first), swap(first), second)


def slope(v):
    sig = jax.nn.sigmoid(v)
    return sig * (1.0 + v * (1.0 - sig))


def silu(v):
    return v * jax.nn.sigmoid(v)


def dot(left, right, dims):
    return lax.dot_general(left, right, (dims, ((), ())), preferred_element_type=F32)


def kernel(
    feat_hbm, cot_hbm, bias_hbm, w1_hbm, w2_hbm,
    in_hbm, one_hbm, two_hbm,
    feat, cot, bias, w1, w2, xa, xn, cn, gn, gc, gp, g3n, g3c, g3p, part, acc,
    own, e1, e1r, e2, e2r, h1, h1r, h2, h2r,
    xs1, xs2, xr2, xt1, xt2, sf1, sf2, sy1, sy2, ry1, ry2,
    featp, cotp, out_in, out_one, out_two, in_sem, out_sem, send_sem, recv_sem,
):
    d = lax.axis_index("dp")
    h = lax.axis_index("height")
    t = lax.axis_index("tensor")
    x = h % NX
    z = h // NX
    k = t // 2
    c = t % 2
    home = c == z
    partner = (1 - z) * NX + x
    here = (d, h, t)
    sibling = (d, h, 2 * k + 1 - c)

    copies = [
        pltpu.make_async_copy(src, dst, in_sem.at[i]) for i, (src, dst) in enumerate(
            [(feat_hbm, feat), (cot_hbm, cot), (bias_hbm, bias), (w2_hbm, w2), (w1_hbm, w1)])
    ]
    for copy in copies:
        copy.start()

    counts = {"send": 0, "recv": 0}

    def reserve(kind, n):
        base = counts[kind]
        counts[kind] = base + n
        return base

    def remote(src, dst, s, r, where):
        return pltpu.make_async_remote_copy(
            src_ref=src, dst_ref=dst, send_sem=send_sem.at[s], recv_sem=recv_sem.at[r],
            device_id=where, device_id_type=MESH,
        )

    unfinished = []

    def post(src, dst, r, where, when=None):
        s = reserve("send", 1)

        def make():
            return remote(src, dst, s, r, where)

        def begin():
            make().start()

        def finish():
            make().wait_send()

        if when is None:
            begin()
        else:
            pl.when(when)(begin)
        unfinished.append((finish, when))

    def finish_all():
        for finish, when in unfinished:
            if when is None:
                finish()
            else:
                pl.when(when)(finish)
        unfinished.clear()

    def await_into(dst, r):
        remote(dst, dst, 0, r, here).wait_recv()

    barrier = pltpu.get_barrier_semaphore()

    def greet(where):
        pl.semaphore_signal(barrier, inc=1, device_id=where, device_id_type=MESH)

    for i in range(NX):
        for j in range(4):
            if i or j:
                greet((d, z * NX + (x + i) % NX, 2 * ((k + j) % 4) + c))
        greet((d, (1 - z) * NX + i, t))
    for i in range(1, NY):
        greet(((d + i) % NY, h, t))
    greet(sibling)

    copies[0].wait()
    copies[1].wait()
    copies[2].wait()
    for r in range(2):
        for f in range(4):
            v = feat[0, f, r].astype(F32)
            v = jnp.concatenate([v[:16], v[16:]], axis=-1)
            featp[r, f] = v
            xa[c, k, 1 + r, f] = silu(v).astype(BF)
            v = cot[0, f, r].astype(F32)
            v = jnp.concatenate([v[:16], v[16:]], axis=-1)
            cotp[r, f] = v
            cn[1 + r, f] = v.astype(BF)
            gc[2 * h + r, f] = v.astype(BF)

    zero_row = jnp.zeros((4, 16, 128), BF)
    @pl.when(h == 0)
    def _():
        for i in range(2):
            for j in range(4):
                xa[i, j, 0] = zero_row
        cn[0] = zero_row
        gn[0] = zero_row

    @pl.when(h == NX * NZ - 1)
    def _():
        for i in range(2):
            for j in range(4):
                xa[i, j, 3] = zero_row
        cn[3] = zero_row
        gn[3] = zero_row

    for ref in (g3c, g3p):
        for i in range(2):
            for j in (0, 17):
                ref[i, j] = jnp.zeros((6, 16, 256), BF)
            for j in (4, 5):
                ref[i, :, j] = jnp.zeros((18, 16, 256), BF)
    acc[...] = jnp.zeros_like(acc)

    pl.semaphore_wait(barrier, NX * 4 - 1 + NX + NY - 1 + 1)

    def spread(rows, dst, first):
        n = rows.shape[0]
        v = rows[...].astype(F32).reshape(64 * n, 128)
        up, down = next_column(v), prev_column(v)
        nothing = jnp.zeros_like(v)
        pieces = (
            (merge(up, v), merge(down, nothing)),
            (merge_high(up, v), merge_high(down, nothing)),
        )
        for half in range(2):
            for side in range(2):
                dst[half, first:first + n, 0:4, :, 128 * side:128 * side + 128] = (
                    pieces[half][side].astype(BF).reshape(n, 4, 16, 128))

    def transposed_conv(w):
        for a, b in sorted(TAPS, reverse=True):
            n = 2 + a
            left = g3n[:, 2 - b:4 - b, 2 - a:4, :, 0:192]
            tap = 3 * (3 * a + b)
            right = w[tap:tap + 3].reshape(192, 512)
            v = dot(left.reshape(64 * n, 192), right, ((1,), (0,)))
            v = v.reshape(2, 2, n, 16, 512)
            if (a, b) == (2, 2):
                part[...] = v
            else:
                part[:, :, 0:n] = part[:, :, 0:n] + v

    def scatter_begin(first, first_in):
        base = reserve("recv", 4)
        for i in range(4):
            low = part[0, :, :, :, 128 * i:128 * i + 128].reshape(128, 128)
            high = part[1, :, :, :, 128 * i:128 * i + 128].reshape(128, 128)
            even, odd = merge(low, high), merge_high(low, high)
            keep = jnp.where(c == 0, even, odd)
            give = jnp.where(c == 0, odd, even)
            own[i] = keep.reshape(2, 4, 16, 128)
            first[i] = give.astype(BF).reshape(2, 4, 16, 128)
            post(first.at[i], first_in.at[i], base + i, sibling)
        return base

    def scatter_on(base, first_in, second, second_in):
        after = reserve("recv", 4)
        for j in (2, 1, 3, 0):
            chip = (k + j) % 4
            await_into(first_in.at[chip], base + chip)
            v = own[chip] + first_in[chip].astype(F32)
            if j:
                second[chip] = v.astype(BF)
                post(second.at[chip], second_in.at[k], after + k, (d, h, 2 * chip + c))
            else:
                own[chip] = v
        return after

    def scatter_end(base, second_in):
        total = own[k]
        for j in range(1, 4):
            chip = (k + j) % 4
            await_into(second_in.at[chip], base + chip)
            total = total + second_in[chip].astype(F32)
        return total

    def near_begin(ref):
        base = reserve("recv", 2)
        post(ref.at[1], ref.at[3], base, (d, h - 1, t), h > 0)
        post(ref.at[2], ref.at[0], base + 1, (d, h + 1, t), h < NX * NZ - 1)
        return base

    def near_end(ref, base):
        @pl.when(h < NX * NZ - 1)
        def _():
            await_into(ref.at[3], base)

        @pl.when(h > 0)
        def _():
            await_into(ref.at[0], base + 1)

    def rows_of(ref, source):
        return ref.at[pl.ds(2 * source, 2)]

    def far_begin(ref):
        base = reserve("recv", 8)
        rows = rows_of(ref, h)
        post(rows, rows, base + h, (d, partner, t))
        for j in (1, 3, 2):
            post(rows, rows, base + h, (d, z * NX + (x + j) % NX, t))
        return base

    def far_relay(ref, base):
        rows = rows_of(ref, partner)
        await_into(rows, base + partner)
        for j in (1, 3, 2):
            post(rows, rows, base + partner, (d, z * NX + (x + j) % NX, t))

    def far_end(ref, base):
        for i in (z, 1 - z):
            for j in range(1, NX):
                other = i * NX + (x + j) % NX
                await_into(rows_of(ref, other), base + other)

    def transposed(packed):
        v = jnp.transpose(packed)
        return jnp.concatenate([v[:64], v[64:]], axis=1).astype(BF).reshape(4, 16, 256)

    def grad_begin(xt, g3, sf, sy, ry, parts):
        base = reserve("recv", 12)
        for a in range(3):
            sides = []
            for b in range(3):
                total = None
                for s in range(NX * NZ):
                    left = xt[s // NX, s % NX].reshape(64, 256)
                    right = g3[:, 2 * s + 2 - b:2 * s + 4 - b, 2 - a:6 - a]
                    v = dot(left, right.reshape(256, 256), ((1,), (0,)))
                    total = v if total is None else total + v
                tile = total[:, 0:128].reshape(4, 16, 128)
                sf[:, a, b] = tile
                sy[:, a, b] = tile.astype(BF)
                sides.append(total[:, 128:256])
            for i, v in ((3, merge(sides[0], sides[1])), (4, sides[2])):
                tile = v.reshape(4, 16, 128)
                sf[:, a, i] = tile
                sy[:, a, i] = tile.astype(BF)
            for first, n in parts:
                if first + n - 1 == a:
                    piece = pl.ds(first, n)
                    for j in (2, 1, 3):
                        other = (d + j) % NY
                        post(sy.at[other, piece], ry.at[d, piece], base + 4 * first + d,
                             (other, h, t))
        return base

    scale = 1.0 / math.sqrt(4 * 4 * 16 * 32)

    def grad_end(base, sf, ry, out, parts):
        for first, n in parts:
            v = sf[d, first:first + n]
            for j in range(1, NY):
                other = (d + j) % NY
                await_into(ry.at[other, pl.ds(first, n)], base + 4 * first + other)
                v = v + ry[other, first:first + n].astype(F32)
            v = v * scale
            for a in range(n):
                for b in range(3):
                    tap = 9 * (first + a) + 3 * b
                    out[tap] = v[a, b, :, 0:64]
                    out[tap + 1] = v[a, b, :, 64:128]
                    side = v[a, 3 + b // 2]
                    out[tap + 2] = side[:, 64:128] if b == 1 else side[:, 0:64]

    a_base = reserve("recv", 8)
    up_base = reserve("recv", 8)
    down_base = reserve("recv", 8)

    not_first, not_last = h > 0, h < NX * NZ - 1

    def halo(chip, up_when, down_when):
        post(xa.at[c, chip, 1], xa.at[c, chip, 3], up_base + 4 * c + chip,
             (d, h - 1, t), up_when)
        post(xa.at[c, chip, 2], xa.at[c, chip, 0], down_base + 4 * c + chip,
             (d, h + 1, t), down_when)

    mine = xa.at[c, k, pl.ds(1, 2)]
    for j in (2, 1, 3):
        post(mine, mine, a_base + 4 * c + k, (d, h, 2 * ((k + j) % 4) + c))
    post(mine, mine, a_base + 4 * c + k, sibling)
    cn_base = near_begin(cn)
    halo(k, not_first, not_last)

    near_end(cn, cn_base)
    spread(cn, g3n, 0)

    for j in (1, 3, 2):
        chip = (k + j) % 4
        rows = xa.at[c, chip, pl.ds(1, 2)]
        await_into(rows, a_base + 4 * c + chip)
        post(rows, rows, a_base + 4 * c + chip, sibling)
        halo(chip, not_first & (h != NX), not_last & (h != NX - 1))

    @pl.when(h == NX)
    def _():
        await_into(xa.at[c, k, 0], down_base + 4 * c + k)

    @pl.when(h == NX - 1)
    def _():
        await_into(xa.at[c, k, 3], up_base + 4 * c + k)

    for j in (2, 1, 3):
        peer = (d, h, 2 * ((k + j) % 4) + c)
        post(xa.at[c, k, 0], xa.at[c, k, 0], down_base + 4 * c + k, peer, h == NX)
        post(xa.at[c, k, 3], xa.at[c, k, 3], up_base + 4 * c + k, peer, h == NX - 1)

    for i in range(4):
        xs1[:, i] = transposed(xa[c, i, 1:3].astype(F32).reshape(128, 128))
    x1_base = reserve("recv", 8)

    @pl.when(home)
    def _():
        xt1[z, x] = xs1[x]

    copies[3].wait()
    transposed_conv(w2)
    e_base = scatter_begin(e1, e1r)
    c_base = far_begin(gc)

    for row, base, when, edge in (
        (3, up_base, not_last, NX - 1), (0, down_base, not_first, NX)
    ):
        for j in range(4):
            chip = (k + j) % 4

            @pl.when(when if j else when & (h != edge))
            def _():
                await_into(xa.at[c, chip, row], base + 4 * c + chip)

    up_sib = reserve("recv", 1)
    post(xa.at[c, :, 3], xa.at[c, :, 3], up_sib, sibling, not_last)
    down_sib = reserve("recv", 1)
    post(xa.at[c, :, 0], xa.at[c, :, 0], down_sib, sibling, not_first)

    e_base = scatter_on(e_base, e1r, e2, e2r)

    for j in range(4):
        chip = (k + j) % 4
        await_into(xa.at[1 - c, chip, pl.ds(1, 2)], a_base + 4 * (1 - c) + chip)

    @pl.when(not_last)
    def _():
        await_into(xa.at[1 - c, :, 3], up_sib)

    @pl.when(not_first)
    def _():
        await_into(xa.at[1 - c, :, 0], down_sib)

    for i in range(4):
        first = xa[0, i].astype(F32).reshape(256, 128)
        second = xa[1, i].astype(F32).reshape(256, 128)
        xn[0, :, :, :, 128 * i:128 * i + 128] = (
            merge(first, second).astype(BF).reshape(4, 4, 16, 128))
        xn[1, :, :, :, 128 * i:128 * i + 128] = (
            merge_high(first, second).astype(BF).reshape(4, 4, 16, 128))

    copies[4].wait()
    for a, b in TAPS:
        n = 2 + a
        left = xn[:, b:b + 2, 0:n].reshape(64 * n, 512)
        tap = 3 * (3 * a + b)
        right = w1[tap:tap + 3].reshape(192, 512)
        v = dot(left, right, ((1,), (1,))).reshape(2, 2, n, 16, 192)
        acc[:, :, 2 - a:4, :, 0:192] = acc[:, :, 2 - a:4, :, 0:192] + v
    low0 = acc[0, :, :, :, 0:128].reshape(128, 128)
    low1 = acc[0, :, :, :, 128:256].reshape(128, 128)
    high0 = acc[1, :, :, :, 0:128].reshape(128, 128)
    high1 = acc[1, :, :, :, 128:256].reshape(128, 128)
    wide_bias = jnp.concatenate([bias[...], bias[...]], axis=1)
    preact = (prev_column(merge(low0, high0)) + merge_high(low0, high0)
              + next_column(merge(low1, high1)) + wide_bias)
    act_two = silu(preact).astype(BF).astype(F32)

    xs2[...] = transposed(act_two)
    x2_cross = reserve("recv", 1)
    x2_base = reserve("recv", 32)
    post(xs2, xr2, x2_cross, (d, partner, t), jnp.logical_not(home))

    def distribute(src, half):
        for i in (0, 1, 3, 2):
            for j in (2, 1, 3, 0):
                if i or j:
                    other, chip = (x + i) % NX, (k + j) % 4
                    post(src.at[other], xt2.at[half, x, k],
                         x2_base + 16 * half + 4 * x + k,
                         (d, z * NX + other, 2 * chip + c), home)

        @pl.when(home)
        def _():
            xt2[half, x, k] = src[x]

    distribute(xs2, z)
    for j in (2, 1, 3, 0):
        other = (x + j) % NX
        post(xs1.at[other], xt1.at[z, x], x1_base + h, (d, c * NX + other, t),
             None if j else jnp.logical_not(home))
    far_relay(gc, c_base)

    grad_pre = scatter_end(e_base, e2r).reshape(128, 128) * slope(preact)
    grad_rows = grad_pre.astype(BF).reshape(2, 4, 16, 128)
    gn[1:3] = grad_rows
    gp[pl.ds(2 * h, 2)] = grad_rows
    gn_base = near_begin(gn)
    p_base = far_begin(gp)

    @pl.when(home)
    def _():
        await_into(xr2, x2_cross)

    distribute(xr2, 1 - z)

    x1_sib = reserve("recv", 8)
    for i in (z, 1 - z):
        for j in range(NX):
            other = (x + j) % NX
            block = xt1.at[i, other]
            source = i * NX + other

            @pl.when(home if j else home & (i != z))
            def _():
                await_into(block, x1_base + source)

        post(xt1.at[i], xt1.at[i], x1_sib + i, sibling, home)

    far_end(gc, c_base)
    spread(gc, g3c, 1)

    near_end(gn, gn_base)
    spread(gn, g3n, 0)
    transposed_conv(w1)
    h_base = scatter_begin(h1, h1r)
    far_relay(gp, p_base)

    x2_sib = reserve("recv", 8)
    for half in (z, 1 - z):
        for i in range(NX):
            other = (x + i) % NX

            @pl.when(home)
            def _():
                for j in range(4):
                    chip = (k + j) % 4
                    if i or j:
                        await_into(xt2.at[half, other, chip],
                                   x2_base + 16 * half + 4 * other + chip)

        post(xt2.at[half], xt2.at[half], x2_sib + half, sibling, home)

    h_base = scatter_on(h_base, h1r, h2, h2r)

    def await_sibling(xt, base):
        @pl.when(jnp.logical_not(home))
        def _():
            for i in range(NZ):
                await_into(xt.at[i], base + i)

    whole, cut = ((0, 3),), ((0, 1), (1, 1), (2, 1))
    await_sibling(xt2, x2_sib)
    y2_base = grad_begin(xt2, g3c, sf2, sy2, ry2, whole)
    far_end(gp, p_base)
    spread(gp, g3p, 1)
    await_sibling(xt1, x1_sib)
    y1_base = grad_begin(xt1, g3p, sf1, sy1, ry1, cut)
    finish_all()

    back = scatter_end(h_base, h2r)
    grad_in = cotp[...] + back * slope(featp[...])
    for r in range(2):
        for f in range(4):
            out_in[0, f, r, 0:16] = grad_in[r, f, :, 0:64].astype(BF)
            out_in[0, f, r, 16:32] = grad_in[r, f, :, 64:128].astype(BF)
    results = [
        pltpu.make_async_copy(src, dst, out_sem.at[i]) for i, (src, dst) in enumerate(
            [(out_in, in_hbm), (out_two, two_hbm), (out_one, one_hbm)])
    ]
    results[0].start()
    grad_end(y2_base, sf2, ry2, out_two, whole)
    results[1].start()
    grad_end(y1_base, sf1, ry1, out_one, cut)
    results[2].start()

    finish_all()
    for copy in results:
        copy.wait()
    assert counts["send"] <= SENDS and counts["recv"] <= RECVS


def write_kernel(a, b, c, a_out, b_out, c_out, a_mid, b_mid, c_mid, in_sem, out_sem):
    stages = []
    for first in range(0, 27, 9):
        part = pl.ds(first, 9)
        stages.append((c.at[part], c_mid.at[part], c_out.at[part]))
        stages.append((b.at[part], b_mid.at[part], b_out.at[part]))
    stages.append((a, a_mid, a_out))
    first = [
        pltpu.make_async_copy(src, mid, in_sem.at[i])
        for i, (src, mid, _) in enumerate(stages)
    ]
    second = [
        pltpu.make_async_copy(mid, dst, out_sem.at[i])
        for i, (_, mid, dst) in enumerate(stages)
    ]
    for copy in first:
        copy.start()
    for copy, after in zip(first, second):
        copy.wait()
        after.start()
    for copy in second:
        copy.wait()


def local(features, cotangent, conv_one, bias_one, conv_two):
    hbm = pl.BlockSpec(memory_space=pltpu.HBM)
    grad_in_shape = (1, 4, 2, 32, 64)
    block = (2, 4, 16, 128)
    blocks = pltpu.VMEM((4,) + block, BF)
    near = pltpu.VMEM((4, 4, 16, 128), BF)
    far = pltpu.VMEM((16, 4, 16, 128), BF)
    wide = pltpu.VMEM((2, 18, 6, 16, 256), BF)
    turned = pltpu.VMEM((4, 16, 256), BF)
    clip = pltpu.VMEM((2, 4, 4, 16, 256), BF)
    sums = pltpu.VMEM((4, 3, 5, 16, 128), F32)
    sent = pltpu.VMEM((4, 3, 5, 16, 128), BF)
    kernel_block = pltpu.VMEM((27, 64, 512), BF)
    scratch = [
        pltpu.VMEM(grad_in_shape, BF), pltpu.VMEM(grad_in_shape, BF),
        pltpu.VMEM((1, 64), F32), kernel_block, kernel_block,
        pltpu.VMEM((2, 4, 4, 4, 16, 128), BF), pltpu.VMEM((2, 4, 4, 16, 512), BF),
        near, near, far, far, pltpu.VMEM((2, 4, 4, 16, 256), BF), wide, wide,
        pltpu.VMEM((2, 2, 4, 16, 512), F32), pltpu.VMEM((2, 2, 4, 16, 256), F32),
        pltpu.VMEM((4,) + block, F32),
        blocks, blocks, blocks, blocks, blocks, blocks, blocks, blocks,
        pltpu.VMEM((4, 4, 16, 256), BF), turned, turned, clip, clip,
        sums, sums, sent, sent, sent, sent,
        pltpu.VMEM(block, F32), pltpu.VMEM(block, F32),
        pltpu.VMEM(grad_in_shape, BF),
        pltpu.VMEM((27, 16, 64), F32), pltpu.VMEM((27, 16, 64), F32),
        pltpu.SemaphoreType.DMA((5,)), pltpu.SemaphoreType.DMA((3,)),
        pltpu.SemaphoreType.DMA((SENDS,)), pltpu.SemaphoreType.DMA((RECVS,)),
    ]
    out_shape = (
        jax.ShapeDtypeStruct(grad_in_shape, BF),
        jax.ShapeDtypeStruct((27, 16, 64), F32),
        jax.ShapeDtypeStruct((27, 16, 64), F32),
    )
    outs = pl.pallas_call(
        kernel,
        out_shape=out_shape,
        in_specs=[hbm, hbm, hbm, hbm, hbm],
        out_specs=(hbm, hbm, hbm),
        scratch_shapes=scratch,
        compiler_params=pltpu.CompilerParams(
            collective_id=0, has_side_effects=True, vmem_limit_bytes=56 * 1024 * 1024
        ),
    )(features, cotangent, bias_one.reshape(1, -1), conv_one, conv_two)
    return pl.pallas_call(
        write_kernel,
        out_shape=out_shape,
        in_specs=[hbm, hbm, hbm],
        out_specs=(hbm, hbm, hbm),
        scratch_shapes=[
            pltpu.VMEM(grad_in_shape, BF),
            pltpu.VMEM((27, 16, 64), F32), pltpu.VMEM((27, 16, 64), F32),
            pltpu.SemaphoreType.DMA((7,)), pltpu.SemaphoreType.DMA((7,)),
        ],
        compiler_params=pltpu.CompilerParams(vmem_limit_bytes=60 * 1024 * 1024),
    )(*outs)


def solution(mesh):
    in_specs = (
        P("dp", None, "height", None, "tensor"),
        P("dp", None, "height", None, "tensor"),
        P(None, "tensor", None),
        P("tensor"),
        P(None, "tensor", None),
    )
    out_specs = (
        P("dp", None, "height", None, "tensor"),
        P(None, ("dp", "height"), "tensor"),
        P(None, ("dp", "height"), "tensor"),
    )
    return jax.shard_map(local, mesh=mesh, in_specs=in_specs, out_specs=out_specs, check_vma=False)
```
